512 devices in a mesh: dp: 16 (over z_lo, y), section: 8 (over x, core), mp: 4 (over z_hi).
Axes of the slice: x: 4, y: 8, z: 8 (z_hi: 4, z_lo: 2; z = z_hi * 2 + z_lo), core: 2. Of those that a mesh axis runs over, the one named last changes fastest.
Arguments:
- queries: bfloat16 [8, 3072, 4096], P('section', 'dp', 'mp'), may hold values from -30 to 30
- grad_context: bfloat16 [8, 3072, 4096], P('section', 'dp', 'mp'), may hold values from -6 to 6
- encodings: bfloat16 [96, 128, 896], P('dp', ('section', 'mp')), may hold values from -6 to 6
- table: int32 [48, 2], P('dp'), may hold values from 0 to 5
- counts: int32 [48], P('dp'), may hold values from 1 to 2
- key_weight: bfloat16 [8, 896, 4096], P('section', 'dp', 'mp'), may hold values from -0.1875 to 0.1875
- value_weight: bfloat16 [8, 896, 4096], P('section', 'dp', 'mp'), may hold values from -0.1875 to 0.1875
Outputs:
- context: bfloat16 [8, 3072, 4096], P('section', 'dp', 'mp')
- grad_queries: bfloat16 [8, 3072, 4096], P('section', 'dp', 'mp')
- key_grad: float32 [8, 896, 4096], P('section', 'dp', 'mp')
- value_grad: float32 [8, 896, 4096], P('section', 'dp', 'mp')
The draws below stay inside these ranges and needn't reach their ends.
All inputs are finite; a program needn't handle non-finite values.
Results may differ from the reference program's by a relative error of at most 0.025.
The reference program's roundings to bfloat16 on the way count: a program that leaves them out, or rounds other values in their place, can miss the bound.
Values may be sent and summed in bfloat16 or wider, within the bound.
A program may use at most 64 MiB of HBM per device.

```python
import jax
import jax.numpy as jnp
from jax import lax

HEADS = 32
HDIM = 128
D = 4096
ENC = 896
BLOCK = 64
NLEN = 128
NEIGH = 2
BLOCKS = 3
SLOTS = 6
TOK_REP = 192
TOKENS = 3072
SLOTS_ALL = 96
LAYERS = 8
N_DP = 16


def draw_queries(key, part):
    key = jax.random.fold_in(key, 11)
    base = jax.random.normal(key, (LAYERS, TOKENS, D), jnp.float32)
    return jnp.clip(base, -6.0, 6.0).astype(jnp.bfloat16)


def set_ends(entries, own_key, smallest, largest):
    dims = entries.shape
    place = [jax.random.randint(jax.random.fold_in(own_key, axis), (), 0, dims[axis]) for axis in range(len(dims))]
    entries = entries.at[tuple(place)].set(smallest)
    longest = dims.index(max(dims))
    place[longest] = (place[longest] + 1) % dims[longest]
    return entries.at[tuple(place)].set(largest)


def levels(key, shape, pieces, smallest, largest):
    def one(position, blocks):
        steps = jax.random.uniform(jax.random.fold_in(jax.random.fold_in(key, 6), position), (blocks,), jnp.float32, smallest / len(pieces), largest / len(pieces))
        return jnp.repeat(jnp.exp(steps), shape[position] // blocks).reshape((-1,) + (1,) * (len(shape) - position - 1))

    factor_of = one(*pieces[0])
    for cut in pieces[1:]:
        factor_of = factor_of * one(*cut)
    return factor_of


def bell_draw(own_key, extent, spread, reach, pieces=(), held_as=jnp.bfloat16):
    result = jax.random.normal(own_key, extent, jnp.float32) * spread
    if len(pieces) > 0:
        result = levels(own_key, extent, pieces, -0.22, 0.18) * result
    return jnp.clip(result, min=-reach, max=reach).astype(held_as)


def setup_inputs(seed: int = 0) -> dict:
    key_list = jax.random.split(jax.random.key(seed), 8)
    return {
        "queries": draw_queries(jax.random.fold_in(key_list[7], 71), 0),
        "grad_context": bell_draw(key_list[1], (LAYERS, TOKENS, D), 1.0, 6.0, ((0, 8), (1, 16), (2, 4))),
        "encodings": bell_draw(key_list[2], (SLOTS_ALL, NLEN, ENC), 1.0, 6.0, ((0, 16), (1, 32))),
        "table": set_ends(jax.random.randint(key_list[3], (TOKENS // BLOCK, NEIGH), 0, SLOTS), jax.random.fold_in(key_list[3], 1), 0, SLOTS - 1).astype(jnp.int32),
        "counts": set_ends(jax.random.randint(key_list[4], (TOKENS // BLOCK,), 1, NEIGH + 1), jax.random.fold_in(key_list[4], 1), 1, NEIGH).astype(jnp.int32),
        "key_weight": bell_draw(key_list[5], (LAYERS, ENC, D), ENC ** -0.5, 0.1875, ((0, 8), (1, 16), (2, 4))),
        "value_weight": bell_draw(key_list[6], (LAYERS, ENC, D), ENC ** -0.5, 0.1875, ((0, 8), (1, 16), (2, 4))),
    }


def attend(query_rows, grad_rows, keys, values, table_rep, count_rep):
    scale = HDIM ** -0.5
    key_heads = keys.reshape(SLOTS, NLEN, HEADS, HDIM)[table_rep].reshape(BLOCKS, NEIGH * NLEN, HEADS, HDIM)
    value_heads = values.reshape(SLOTS, NLEN, HEADS, HDIM)[table_rep].reshape(BLOCKS, NEIGH * NLEN, HEADS, HDIM)
    query_heads = query_rows.reshape(BLOCKS, BLOCK, HEADS, HDIM).astype(jnp.float32)
    grad_heads = grad_rows.reshape(BLOCKS, BLOCK, HEADS, HDIM).astype(jnp.float32)
    key_f = key_heads.astype(jnp.float32)
    value_f = value_heads.astype(jnp.float32)
    scores = jnp.einsum("cqhd,ckhd->chqk", query_heads, key_f) * scale
    live = jnp.arange(NEIGH)[None, :] < count_rep[:, None]
    live = jnp.repeat(live, NLEN, axis=1)
    scores = jnp.where(live[:, None, None, :], scores, jnp.float32(-1e30))
    top = jnp.max(scores, axis=-1, keepdims=True)
    weights = jnp.exp(scores - top)
    probs = weights / jnp.sum(weights, axis=-1, keepdims=True)
    probs_low = probs.astype(jnp.bfloat16).astype(jnp.float32)
    context = jnp.einsum("chqk,ckhd->cqhd", probs_low, value_f).reshape(TOK_REP, D).astype(jnp.bfloat16)
    dprob = jnp.einsum("cqhd,ckhd->chqk", grad_heads, value_f)
    delta = jnp.sum(probs * dprob, axis=-1, keepdims=True)
    dscore = (probs * (dprob - delta) * scale).astype(jnp.bfloat16).astype(jnp.float32)
    grad_queries = jnp.einsum("chqk,ckhd->cqhd", dscore, key_f).reshape(TOK_REP, D).astype(jnp.bfloat16)
    key_terms = jnp.einsum("chqk,cqhd->ckhd", dscore, query_heads).reshape(BLOCKS, NEIGH, NLEN, D)
    value_terms = jnp.einsum("chqk,cqhd->ckhd", probs_low, grad_heads).reshape(BLOCKS, NEIGH, NLEN, D)
    onehot = (table_rep[:, :, None] == jnp.arange(SLOTS)[None, None, :]).astype(jnp.float32)
    key_slots = jnp.einsum("cjs,cjnm->snm", onehot, key_terms, precision=lax.Precision.HIGHEST)
    value_slots = jnp.einsum("cjs,cjnm->snm", onehot, value_terms, precision=lax.Precision.HIGHEST)
    key_slots = key_slots.reshape(SLOTS * NLEN, D).astype(jnp.bfloat16)
    value_slots = value_slots.reshape(SLOTS * NLEN, D).astype(jnp.bfloat16)
    return context, grad_queries, key_slots, value_slots


def reference(queries, grad_context, encodings, table, counts, key_weight, value_weight):
    enc_all = encodings.reshape(N_DP, SLOTS * NLEN, ENC)
    table_all = table.reshape(N_DP, BLOCKS, NEIGH)
    count_all = counts.reshape(N_DP, BLOCKS)
    contexts, grads_q, key_grads, value_grads = [], [], [], []
    for layer in range(LAYERS):
        query_all = queries[layer].reshape(N_DP, TOK_REP, D)
        grad_all = grad_context[layer].reshape(N_DP, TOK_REP, D)
        wk = key_weight[layer]
        wv = value_weight[layer]

        def one_replica(items):
            flat, query_rows, grad_rows, table_rep, count_rep = items
            keys = jnp.dot(flat, wk, preferred_element_type=jnp.float32).astype(jnp.bfloat16)
            values = jnp.dot(flat, wv, preferred_element_type=jnp.float32).astype(jnp.bfloat16)
            context, grad_queries, key_slots, value_slots = attend(query_rows, grad_rows, keys, values, table_rep, count_rep)
            key_term = jnp.dot(flat.T, key_slots, preferred_element_type=jnp.float32).astype(jnp.bfloat16)
            value_term = jnp.dot(flat.T, value_slots, preferred_element_type=jnp.float32).astype(jnp.bfloat16)
            return context, grad_queries, key_term, value_term

        context, grad_queries, key_term, value_term = lax.map(one_replica, (enc_all, query_all, grad_all, table_all, count_all))
        contexts.append(context.reshape(TOKENS, D))
        grads_q.append(grad_queries.reshape(TOKENS, D))
        key_grads.append(jnp.sum(key_term.astype(jnp.float32), axis=0))
        value_grads.append(jnp.sum(value_term.astype(jnp.float32), axis=0))
    return jnp.stack(contexts), jnp.stack(grads_q), jnp.stack(key_grads), jnp.stack(value_grads)
```

```python
import functools

import jax
import jax.numpy as jnp
import numpy as np
from jax import lax
from jax.experimental import pallas as pl
from jax.experimental.pallas import tpu as pltpu
from jax.sharding import PartitionSpec as P

MESH = pl.DeviceIdType.MESH
F32, BF16 = jnp.float32, jnp.bfloat16
HDIM = 128
LOG2E = 1.4426950408889634
NY, NX, NZH, NZ = 8, 4, 4, 8
HEADS = 4
SLOTS, PIECE, ENC = 6, 4, 896
CHUNK = SLOTS * PIECE
TOKENS = 768
ROWS, BLOCK, BLOCKS = 192, 64, 3
WROWS = 56
ZORDER = (0, 1, 7, 2, 6, 3, 5, 4)


def mod(value, n):
    return lax.rem(value + n, n)


def kernel(
    table_ref, counts_ref, slot_ref, q_ref, g_ref, enc_ref, wk_ref, wv_ref,
    ctx_out, gq_out, kg_out, vg_out,
    ebuf, tok, tok_t, wraw, qg, mult, keys, values, probs_s, dscore_s, slots_s, terms, landed, stage, total,
    mult_sem, z_send, z_recv, xp_send, xp_recv, xm_send, xm_recv, xo_send, xo_recv, sib_send, sib_recv,
    wl_sem, wz_send, wz_recv, wy_send, wy_recv, ql_sem, qz_send, qz_recv, rs_send, rs_recv,
    ol_sem, oz_send, oz_recv, fl_sem, fz_send, fz_recv,
):
    dp, section, zh = lax.axis_index("dp"), lax.axis_index("section"), lax.axis_index("mp")
    zl, y = dp // NY, lax.rem(dp, NY)
    x, core = section // 2, lax.rem(section, 2)
    z = zh * 2 + zl
    other = 1 - zl

    partner = {"dp": other * NY + y}
    sibling = {"section": x * 2 + 1 - core}

    def at_y(step):
        return {"dp": zl * NY + mod(y + step, NY)}

    def at_x(step):
        return {"section": mod(x + step, NX) * 2 + core}

    def at_z(step):
        there = mod(z + step, NZ)
        return {"dp": lax.rem(there, 2) * NY + y, "mp": there // 2}

    def remote(src, dst, send, recv, device):
        return pltpu.make_async_remote_copy(
            src_ref=src, dst_ref=dst, send_sem=send, recv_sem=recv, device_id=device, device_id_type=MESH
        )

    sent = []

    def push(src, dst, send, recv, device):
        copy = remote(src, dst, send, recv, device)
        copy.start()
        sent.append(copy)

    def arrived(ref, recv):
        remote(ref, ref, recv, recv, sibling).wait_recv()

    barrier = pltpu.get_barrier_semaphore()
    friends = [at_z(d) for d in range(1, NZ)] + [at_x(1), at_x(-1), sibling, at_y(1), at_y(-1)]
    for friend in friends:
        pl.semaphore_signal(barrier, inc=1, device_id=friend, device_id_type=MESH)

    def own_columns(h):
        return pl.ds(pl.multiple_of(zl * HEADS * HDIM + h * HDIM, HDIM), HDIM)

    def other_columns(h):
        return pl.ds(pl.multiple_of(other * HEADS * HDIM + h * HDIM, HDIM), HDIM)

    local = []
    for h in range(HEADS):
        for i, w_ref in enumerate((wk_ref, wv_ref)):
            copy = pltpu.make_async_copy(
                w_ref.at[0, :, own_columns(h)], wraw.at[h, zl, y, :, pl.ds(i * HDIM, HDIM)], wl_sem.at[h, i]
            )
            copy.start()
            local.append(copy)
    local_q = []
    for h in range(HEADS):
        for i, w_ref in enumerate((q_ref, g_ref)):
            copy = pltpu.make_async_copy(w_ref.at[0, :, own_columns(h)], qg.at[0, h, i], ql_sem.at[h, i])
            copy.start()
            local_q.append(copy)
    pieces = [enc_ref[s].astype(F32) for s in range(SLOTS)]
    ebuf[zl, zh, x, core] = jnp.concatenate(pieces, axis=0).astype(BF16)
    slot_of = slot_ref[...]
    for c in range(BLOCKS):
        times = jnp.where(slot_of == table_ref[c, 0], 1.0, 0.0)
        second = jnp.where(counts_ref[c] > 1, 1.0, 0.0)
        mult[0, c] = times + jnp.where(slot_of == table_ref[c, 1], 1.0, 0.0) * second

    pl.semaphore_wait(barrier, len(friends))

    def chunk(dz, dx, core_of):
        zz = mod(z + dz, NZ)
        return ebuf.at[lax.rem(zz, 2), zz // 2, mod(x + dx, NX), core_of]

    mine = chunk(0, 0, core)
    for d in ZORDER[1:]:
        push(mine, mine, z_send.at[d], z_recv.at[d], at_z(d))
    for h in range(HEADS):
        for i, w_ref in enumerate((wk_ref, wv_ref)):
            push(
                w_ref.at[0, :, other_columns(h)], wraw.at[h, zl, y, :, pl.ds(i * HDIM, HDIM)],
                wz_send.at[h, i], wz_recv.at[h, i], partner,
            )
    push(mult.at[0], mult.at[1], mult_sem.at[0], mult_sem.at[1], partner)
    for h in range(HEADS):
        for i, w_ref in enumerate((q_ref, g_ref)):
            push(w_ref.at[0, :, other_columns(h)], qg.at[1, h, i], qz_send.at[h, i], qz_recv.at[h, i], partner)

    def w_step(h, t):
        way = 1 if h % 2 == 0 else -1
        if t == 0:
            for i in range(2):
                local[h * 2 + i].wait()
                arrived(wraw.at[h, other, y, :, pl.ds(i * HDIM, HDIM)], wz_recv.at[h, i])
        else:
            arrived(wraw.at[h, :, mod(y - way * t, NY)], wy_recv.at[h, t - 1])
        if t < 4:
            there = wraw.at[h, :, mod(y - way * t, NY)]
            push(there, there, wy_send.at[h, t], wy_recv.at[h, t], at_y(way))
        if 0 < t < 4:
            arrived(wraw.at[h, :, mod(y + way * t, NY)], wy_recv.at[h, 3 + t])
        if t < 3:
            there = wraw.at[h, :, mod(y + way * t, NY)]
            push(there, there, wy_send.at[h, 4 + t], wy_recv.at[h, 4 + t], at_y(-way))

    def to_sibling(ref, d, dx):
        i = d * NX + dx
        push(ref, ref, sib_send.at[i], sib_recv.at[i], sibling)

    def e_first(d):
        ref = chunk(-d, 0, core)
        if d:
            arrived(ref, z_recv.at[d])
        push(ref, ref, xp_send.at[d], xp_recv.at[d], at_x(1))
        push(ref, ref, xm_send.at[d], xm_recv.at[d], at_x(-1))
        to_sibling(ref, d, 0)

    def e_second(d):
        ref = chunk(-d, -1, core)
        arrived(ref, xp_recv.at[d])
        if d % 2 == 0:
            push(ref, ref, xo_send.at[d], xo_recv.at[d], at_x(1))
        to_sibling(ref, d, 3)
        ref = chunk(-d, 1, core)
        arrived(ref, xm_recv.at[d])
        if d % 2 == 1:
            push(ref, ref, xo_send.at[d], xo_recv.at[d], at_x(-1))
        to_sibling(ref, d, 1)

    def e_third(d):
        ref = chunk(-d, 2, core)
        arrived(ref, xo_recv.at[d])
        to_sibling(ref, d, 2)

    turns = [(0,), (1, 7), (2, 6), (3, 5), (4,)]
    w_turns = [
        [(0, 0), (1, 0)], [(0, 1), (1, 1)], [(0, 2), (1, 2)], [(0, 3), (1, 3), (2, 0)], [(0, 4), (1, 4), (3, 0)],
        [(2, 1), (3, 1)], [(2, 2), (3, 2)], [(2, 3), (3, 3)], [(2, 4), (3, 4)],
    ]
    for turn in range(9):
        for stage_of, behind in ((e_first, 0), (e_second, 2), (e_third, 4)):
            if 0 <= turn - behind < len(turns):
                for d in turns[turn - behind]:
                    stage_of(d)
        for h, t in w_turns[turn]:
            w_step(h, t)
    for d in range(NZ):
        for dx in range(NX):
            arrived(chunk(-d, dx, 1 - core), sib_recv.at[d * NX + dx])
    for copy in local_q:
        copy.wait()
    for h in range(HEADS):
        for i in range(2):
            arrived(qg.at[1, h, i], qz_recv.at[h, i])
    arrived(mult.at[1], mult_sem.at[1])

    for r in range(2):

        @pl.loop(0, NZH)
        def _(zz):
            part = ebuf[r, zz].reshape(NX * 2, CHUNK, ENC).astype(F32).reshape(NX * 2 * CHUNK, ENC)
            span = pl.ds(pl.multiple_of(zz * NX * 2 * CHUNK, NX * 2 * CHUNK), NX * 2 * CHUNK)
            tok[r, span, :] = part.astype(BF16)

        @pl.loop(0, 7)
        def _(i):
            span = pl.ds(pl.multiple_of(i * HDIM, HDIM), HDIM)
            tok_t[r, span, :] = tok[r, :, span].T

    scale = HDIM**-0.5

    def project(h):
        w = wraw[h].reshape(2 * NY * WROWS, 2 * HDIM)
        for r in range(2):

            @pl.loop(0, 3)
            def _(i):
                span = pl.ds(pl.multiple_of(i * 256, 256), 256)
                kv = jnp.dot(tok[r, span, :], w, preferred_element_type=F32).astype(BF16)
                keys[r, span, :] = kv[:, :HDIM]
                values[r, span, :] = kv[:, HDIM:]

    def nt(a, b):
        return lax.dot_general(a, b, (((1,), (1,)), ((), ())), preferred_element_type=F32)

    def tn(a, b):
        return lax.dot_general(a, b, (((0,), (0,)), ((), ())), preferred_element_type=F32)

    def attend(h, near):
        r = zl if near == 0 else other

        @pl.loop(0, BLOCKS)
        def _(c):
            k, v = keys[r], values[r]
            span = pl.ds(pl.multiple_of(c * BLOCK, BLOCK), BLOCK)
            q, g = qg[near, h, 0, span, :], qg[near, h, 1, span, :]
            m = mult[near, c, pl.ds(0, 1), :]
            scores = nt(q, k) + jnp.where(m > 0.0, 0.0, -1e30)
            top = jnp.max(scores, axis=1, keepdims=True)
            weights = jnp.exp2((scores - top) * (scale * LOG2E)) * m
            probs = weights / jnp.sum(weights, axis=1, keepdims=True)
            probs_s[span, :] = probs.astype(BF16)
            dprob = nt(g, v)
            delta = jnp.sum(probs * dprob, axis=1, keepdims=True)
            dscore_s[span, :] = (probs * (dprob - delta) * scale).astype(BF16)

        k, v = keys[r], values[r]
        p, s = probs_s[...], dscore_s[...]
        q, g = qg[near, h, 0], qg[near, h, 1]
        stage[near, h, 0] = jnp.dot(p, v, preferred_element_type=F32).astype(BF16)
        stage[near, h, 1] = jnp.dot(s, k, preferred_element_type=F32).astype(BF16)
        slots_s[r, :, pl.ds(0, HDIM)] = tn(s, q).astype(BF16)
        slots_s[r, :, pl.ds(HDIM, HDIM)] = tn(p, g).astype(BF16)
        for i, out in enumerate((ctx_out, gq_out)):
            there = out.at[0, :, own_columns(h)]
            if near:
                push(stage.at[1, h, i], there, oz_send.at[h, i], oz_recv.at[h, i], partner)
            else:
                copy = pltpu.make_async_copy(stage.at[0, h, i], there, ol_sem.at[h, i])
                copy.start()
                ends.append(copy)

    ends = []

    def term(h):
        for half in range(2):
            span = pl.ds(half * NY * WROWS, NY * WROWS)
            both = jnp.dot(tok_t[0, span, :], slots_s[0], preferred_element_type=F32)
            both += jnp.dot(tok_t[1, span, :], slots_s[1], preferred_element_type=F32)
            terms[h, half] = both.reshape(NY, WROWS, 2 * HDIM).astype(BF16)

    def rs_step(h, t):
        way = 1 if h % 2 == 0 else -1
        if t < 4:
            there = mod(y + way * (4 - t), NY)
            if t > 0:
                arrived(landed.at[h, t - 1], rs_recv.at[h, t - 1])
                terms[h, :, there] = (terms[h, :, there].astype(F32) + landed[h, t - 1].astype(F32)).astype(BF16)
            push(terms.at[h, :, there], landed.at[h, t], rs_send.at[h, t], rs_recv.at[h, t], at_y(way))
        if t < 3:
            there = mod(y - way * (3 - t), NY)
            if t > 0:
                arrived(landed.at[h, 3 + t], rs_recv.at[h, 3 + t])
                terms[h, :, there] = (terms[h, :, there].astype(F32) + landed[h, 3 + t].astype(F32)).astype(BF16)
            push(terms.at[h, :, there], landed.at[h, 4 + t], rs_send.at[h, 4 + t], rs_recv.at[h, 4 + t], at_y(-way))
        if t == 4:
            arrived(landed.at[h, 3], rs_recv.at[h, 3])
            arrived(landed.at[h, 6], rs_recv.at[h, 6])
            total[h] = terms[h, :, y].astype(F32) + landed[h, 3].astype(F32) + landed[h, 6].astype(F32)
            for i, out in enumerate((kg_out, vg_out)):
                there = out.at[0, :, own_columns(h)]
                half = pl.ds(i * HDIM, HDIM)
                push(total.at[h, other, :, half], there, fz_send.at[h, i], fz_recv.at[h, i], partner)
                copy = pltpu.make_async_copy(total.at[h, zl, :, half], there, fl_sem.at[h, i])
                copy.start()
                ends.append(copy)

    for h in range(HEADS):
        project(h)
        if h:
            rs_step(h - 1, 1)
        attend(h, 1)
        if h:
            rs_step(h - 1, 2)
        attend(h, 0)
        if h:
            rs_step(h - 1, 3)
        term(h)
        if h:
            rs_step(h - 1, 4)
        rs_step(h, 0)
    for t in range(1, 5):
        rs_step(HEADS - 1, t)

    for h in range(HEADS):
        for i, (out, grad) in enumerate(((ctx_out, kg_out), (gq_out, vg_out))):
            arrived(out.at[0, :, other_columns(h)], oz_recv.at[h, i])
            arrived(grad.at[0, :, other_columns(h)], fz_recv.at[h, i])
    for copy in ends:
        copy.wait()
    for copy in sent:
        copy.wait_send()


def body(queries, grad_context, encodings, table, counts, key_weight, value_weight):
    slot_of = np.broadcast_to((np.arange(TOKENS) % CHUNK // PIECE).astype(np.int32), (8, TOKENS))
    any_ref = pl.BlockSpec(memory_space=pl.ANY)
    vmem = pl.BlockSpec(memory_space=pltpu.VMEM)
    smem = pl.BlockSpec(memory_space=pltpu.SMEM)
    dma = pltpu.SemaphoreType.DMA
    ring = dma((HEADS, 7))
    pair = dma((HEADS, 2))
    eight = dma((NZ,))
    local = key_weight.shape[2]
    scratch = [
        pltpu.VMEM((2, NZH, NX, 2, CHUNK, ENC), BF16),
        pltpu.VMEM((2, TOKENS, ENC), BF16),
        pltpu.VMEM((2, ENC, TOKENS), BF16),
        pltpu.VMEM((HEADS, 2, NY, WROWS, 2 * HDIM), BF16),
        pltpu.VMEM((2, HEADS, 2, ROWS, HDIM), BF16),
        pltpu.VMEM((2, BLOCKS, 8, TOKENS), F32),
        pltpu.VMEM((2, TOKENS, HDIM), BF16),
        pltpu.VMEM((2, TOKENS, HDIM), BF16),
        pltpu.VMEM((ROWS, TOKENS), BF16),
        pltpu.VMEM((ROWS, TOKENS), BF16),
        pltpu.VMEM((2, TOKENS, 2 * HDIM), BF16),
        pltpu.VMEM((HEADS, 2, NY, WROWS, 2 * HDIM), BF16),
        pltpu.VMEM((HEADS, 7, 2, WROWS, 2 * HDIM), BF16),
        pltpu.VMEM((2, HEADS, 2, ROWS, HDIM), BF16),
        pltpu.VMEM((HEADS, 2, WROWS, 2 * HDIM), F32),
        dma((2,)), eight, eight, eight, eight, eight, eight, eight, eight, dma((NZ * NX,)), dma((NZ * NX,)),
        pair, pair, pair, ring, ring, pair, pair, pair, ring, ring,
        pair, pair, pair, pair, pair, pair,
    ]
    return pl.pallas_call(
        kernel,
        out_shape=(
            jax.ShapeDtypeStruct((1, ROWS, local), BF16),
            jax.ShapeDtypeStruct((1, ROWS, local), BF16),
            jax.ShapeDtypeStruct((1, WROWS, local), F32),
            jax.ShapeDtypeStruct((1, WROWS, local), F32),
        ),
        in_specs=[smem, smem, vmem, any_ref, any_ref, vmem, any_ref, any_ref],
        out_specs=(any_ref,) * 4,
        scratch_shapes=scratch,
        compiler_params=pltpu.CompilerParams(
            collective_id=0, has_side_effects=True, vmem_limit_bytes=56 * 1024 * 1024
        ),
    )(table, counts, slot_of, queries, grad_context, encodings, key_weight, value_weight)


def solution(mesh):
    in_specs = (
        P("section", "dp", "mp"),
        P("section", "dp", "mp"),
        P("dp", ("section", "mp"), None),
        P("dp", None),
        P("dp"),
        P("section", "dp", "mp"),
        P("section", "dp", "mp"),
    )
    out_specs = (
        P("section", "dp", "mp"),
        P("section", "dp", "mp"),
        P("section", "dp", "mp"),
        P("section", "dp", "mp"),
    )
    return jax.shard_map(body, mesh=mesh, in_specs=in_specs, out_specs=out_specs, check_vma=False)
```

```python
import functools

import jax
import jax.numpy as jnp
from jax import lax
from jax.experimental import pallas as pl
from jax.experimental.pallas import tpu as pltpu
from jax.sharding import PartitionSpec as P

MESH = pl.DeviceIdType.MESH
F32, BF16 = jnp.float32, jnp.bfloat16
HDIM = 128
LOG2E = 1.4426950408889634
NY, NX, NZH, NZ = 8, 4, 4, 8
HEADS = 4
SLOTS, PIECE, ENC = 6, 4, 896
CHUNK = SLOTS * PIECE
TOKENS = 768
ROWS, BLOCK, BLOCKS = 192, 64, 3
WROWS = 56


def mod(value, n):
    return lax.rem(value + n, n)


def kernel(
    table_ref, counts_ref, q_ref, g_ref, enc_ref, wk_ref, wv_ref,
    ctx_out, gq_out, kg_out, vg_out,
    ebuf, tok, wraw, qg, mult, times, keys, values, slots_t, terms, landed, stage, total,
    mult_sem, z_send, z_recv, xp_send, xp_recv, xm_send, xm_recv, xo_send, xo_recv, sib_send, sib_recv,
    wl_sem, wz_send, wz_recv, wy_send, wy_recv, ql_sem, qz_send, qz_recv, rs_send, rs_recv,
    ol_sem, oz_send, oz_recv, fl_sem, fz_send, fz_recv,
):
    dp, section, zh = lax.axis_index("dp"), lax.axis_index("section"), lax.axis_index("mp")
    zl, y = dp // NY, lax.rem(dp, NY)
    x, core = section // 2, lax.rem(section, 2)
    z = zh * 2 + zl
    other = 1 - zl

    partner = {"dp": other * NY + y}
    sibling = {"section": x * 2 + 1 - core}

    def at_y(step):
        return {"dp": zl * NY + mod(y + step, NY)}

    def at_x(step):
        return {"section": mod(x + step, NX) * 2 + core}

    def at_z(step):
        there = mod(z + step, NZ)
        return {"dp": lax.rem(there, 2) * NY + y, "mp": there // 2}

    def remote(src, dst, send, recv, device):
        return pltpu.make_async_remote_copy(
            src_ref=src, dst_ref=dst, send_sem=send, recv_sem=recv, device_id=device, device_id_type=MESH
        )

    sent = []

    def push(src, dst, send, recv, device):
        copy = remote(src, dst, send, recv, device)
        copy.start()
        sent.append(copy)

    def arrived(ref, recv):
        remote(ref, ref, recv, recv, sibling).wait_recv()

    barrier = pltpu.get_barrier_semaphore()
    friends = [at_z(d) for d in (1, -1, 2, -2)] + [at_y(d) for d in (1, -1, 2, -2)] + [at_x(1), at_x(-1), sibling]
    for friend in friends:
        pl.semaphore_signal(barrier, inc=1, device_id=friend, device_id_type=MESH)

    def own_columns(h):
        return pl.ds(pl.multiple_of(zl * HEADS * HDIM + h * HDIM, HDIM), HDIM)

    def other_columns(h):
        return pl.ds(pl.multiple_of(other * HEADS * HDIM + h * HDIM, HDIM), HDIM)

    local = []
    for h in range(HEADS):
        for i, w_ref in enumerate((wk_ref, wv_ref)):
            copy = pltpu.make_async_copy(
                w_ref.at[0, :, own_columns(h)], wraw.at[h, zl, y, :, pl.ds(i * HDIM, HDIM)], wl_sem.at[h, i]
            )
            copy.start()
            local.append(copy)
    local_q = []
    for h in range(HEADS):
        for i, w_ref in enumerate((q_ref, g_ref)):
            copy = pltpu.make_async_copy(w_ref.at[0, :, own_columns(h)], qg.at[0, h, i], ql_sem.at[h, i])
            copy.start()
            local_q.append(copy)
    pieces = [enc_ref[s].astype(F32) for s in range(SLOTS)]
    ebuf[zl, zh, x, core] = jnp.concatenate(pieces, axis=0).astype(BF16)
    token = lax.broadcasted_iota(jnp.int32, (8, TOKENS), 1)
    slot_of = (token - CHUNK * ((token * 2731) >> 16)) >> 2
    row = lax.broadcasted_iota(jnp.int32, (8, TOKENS), 0)
    compact = jnp.zeros((8, TOKENS), F32)
    for c in range(BLOCKS):
        first = jnp.where(slot_of == table_ref[pl.ds(0, 1), pl.ds(c, 1)], 1.0, 0.0)
        second = jnp.where(slot_of == table_ref[pl.ds(1, 1), pl.ds(c, 1)], 1.0, 0.0)
        both = first + second * jnp.where(counts_ref[c] > 1, 1.0, 0.0)
        compact = jnp.where(row == c, both, compact)
    mult[0] = compact

    pl.semaphore_wait(barrier, len(friends))

    def chunk(dz, dx, core_of):
        zz = mod(z + dz, NZ)
        return ebuf.at[lax.rem(zz, 2), zz // 2, mod(x + dx, NX), core_of]

    mine = chunk(0, 0, core)
    for d in (1, 7, 2, 6):
        push(mine, mine, z_send.at[d], z_recv.at[d], at_z(d if d < 4 else d - NZ))

    def send_weights():
        for h in range(HEADS):
            for i, w_ref in enumerate((wk_ref, wv_ref)):
                push(
                    w_ref.at[0, :, other_columns(h)], wraw.at[h, zl, y, :, pl.ds(i * HDIM, HDIM)],
                    wz_send.at[h, i], wz_recv.at[h, i], partner,
                )

    def send_rows():
        push(mult.at[0], mult.at[1], mult_sem.at[0], mult_sem.at[1], partner)
        for h in range(HEADS):
            for i, w_ref in enumerate((q_ref, g_ref)):
                push(w_ref.at[0, :, other_columns(h)], qg.at[1, h, i], qz_send.at[h, i], qz_recv.at[h, i], partner)

    def w_own(h):
        for i in range(2):
            local[h * 2 + i].wait()
            arrived(wraw.at[h, other, y, :, pl.ds(i * HDIM, HDIM)], wz_recv.at[h, i])

    def w_step(h, t):
        way = 1 if h % 2 == 0 else -1
        if t == 0:
            w_own(h)
        else:
            arrived(wraw.at[h, :, mod(y - way * t, NY)], wy_recv.at[h, t - 1])
        if t < 4:
            there = wraw.at[h, :, mod(y - way * t, NY)]
            push(there, there, wy_send.at[h, t], wy_recv.at[h, t], at_y(way))
        if 0 < t < 4:
            arrived(wraw.at[h, :, mod(y + way * t, NY)], wy_recv.at[h, 3 + t])
        if t < 3:
            there = wraw.at[h, :, mod(y + way * t, NY)]
            push(there, there, wy_send.at[h, 4 + t], wy_recv.at[h, 4 + t], at_y(-way))

    def to_sibling(ref, d, dx):
        i = d * NX + dx
        push(ref, ref, sib_send.at[i], sib_recv.at[i], sibling)

    def e_first(d):
        ref = chunk(-d, 0, core)
        if d:
            arrived(ref, z_recv.at[d])
        if d == 2:
            push(ref, ref, z_send.at[4], z_recv.at[4], at_z(2))
            push(ref, ref, z_send.at[3], z_recv.at[3], at_z(1))
        if d == 6:
            push(ref, ref, z_send.at[5], z_recv.at[5], at_z(-1))
        push(ref, ref, xp_send.at[d], xp_recv.at[d], at_x(1))
        push(ref, ref, xm_send.at[d], xm_recv.at[d], at_x(-1))
        to_sibling(ref, d, 0)

    def e_second(d):
        ref = chunk(-d, -1, core)
        arrived(ref, xp_recv.at[d])
        if d % 2 == 0:
            push(ref, ref, xo_send.at[d], xo_recv.at[d], at_x(1))
        to_sibling(ref, d, 3)
        ref = chunk(-d, 1, core)
        arrived(ref, xm_recv.at[d])
        if d % 2 == 1:
            push(ref, ref, xo_send.at[d], xo_recv.at[d], at_x(-1))
        to_sibling(ref, d, 1)

    def e_third(d):
        ref = chunk(-d, 2, core)
        arrived(ref, xo_recv.at[d])
        to_sibling(ref, d, 2)

    def w_slot(t):
        for h in range(3):
            w_step(h, t)
        if t >= 3:
            w_step(3, t - 3)

    def each(f, *offsets):
        for d in offsets:
            f(d)

    e_first(0)
    send_weights()
    each(e_first, 1, 7)
    w_slot(0)
    e_second(0)
    each(e_first, 2, 6)
    send_rows()
    each(e_second, 1, 7)
    e_third(0)
    w_slot(1)
    each(e_second, 2, 6)
    each(e_first, 3, 5, 4)
    each(e_third, 1, 7)
    each(e_second, 3, 5)
    each(e_third, 2, 6)
    w_slot(2)
    e_second(4)
    each(e_third, 3, 5, 4)
    w_slot(3)
    for d in range(NZ):
        for dx in range(NX):
            arrived(chunk(-d, dx, 1 - core), sib_recv.at[d * NX + dx])
    for copy in local_q:
        copy.wait()
    for h in range(HEADS):
        for i in range(2):
            arrived(qg.at[1, h, i], qz_recv.at[h, i])
    arrived(mult.at[1], mult_sem.at[1])

    for near in range(2):
        for c in range(BLOCKS):
            times[near, c] = jnp.broadcast_to(mult[near, pl.ds(c, 1), :], (8, TOKENS))

    for r in range(2):

        @pl.loop(0, NZH)
        def _(zz):
            part = ebuf[r, zz].reshape(NX * 2, CHUNK, ENC).astype(F32).reshape(NX * 2 * CHUNK, ENC)
            span = pl.ds(pl.multiple_of(zz * NX * 2 * CHUNK, NX * 2 * CHUNK), NX * 2 * CHUNK)
            tok[r, span, :] = part.astype(BF16)

    scale = HDIM**-0.5

    def project(h):
        @pl.loop(0, 2)
        def _(r):
            kv = jnp.dot(tok[r], wraw[h].reshape(2 * NY * WROWS, 2 * HDIM), preferred_element_type=F32).astype(BF16)
            keys[r] = kv[:, :HDIM]
            values[r] = kv[:, HDIM:]

    def nt(a, b):
        return lax.dot_general(a, b, (((1,), (1,)), ((), ())), preferred_element_type=F32)

    def tn(a, b):
        return lax.dot_general(a, b, (((0,), (0,)), ((), ())), preferred_element_type=F32)

    def attend(h, near):
        r = zl if near == 0 else other
        k, v = keys[r], values[r]
        q, g = qg[near, h, 0], qg[near, h, 1]
        shape = (BLOCKS, BLOCK // 8, 8, TOKENS)
        m = times[near].reshape(BLOCKS, 1, 8, TOKENS)
        scores = nt(q, k).reshape(shape) + jnp.where(m > 0.0, 0.0, -1e30)
        top = jnp.max(scores, axis=3, keepdims=True)
        weights = jnp.exp2((scores - top) * (scale * LOG2E)) * m
        probs = weights * (1.0 / jnp.sum(weights, axis=3, keepdims=True))
        dprob = nt(g, v).reshape(shape)
        delta = jnp.sum(probs * dprob, axis=3, keepdims=True)
        s = (probs * ((dprob - delta) * scale)).reshape(ROWS, TOKENS).astype(BF16)
        p = probs.reshape(ROWS, TOKENS).astype(BF16)
        stage[near, h, 0] = jnp.dot(p, v, preferred_element_type=F32).astype(BF16)
        stage[near, h, 1] = jnp.dot(s, k, preferred_element_type=F32).astype(BF16)
        slots_t[near, pl.ds(0, HDIM), :] = tn(q, s).astype(BF16)
        slots_t[near, pl.ds(HDIM, HDIM), :] = tn(g, p).astype(BF16)

    def send_out(h):
        for i, out in enumerate((ctx_out, gq_out)):
            there = out.at[0, :, own_columns(h)]
            push(stage.at[1, h, i], there, oz_send.at[h, i], oz_recv.at[h, i], partner)
            copy = pltpu.make_async_copy(stage.at[0, h, i], there, ol_sem.at[h, i])
            copy.start()
            ends.append(copy)

    ends = []

    def term(h):
        both = jnp.dot(slots_t[0], tok[zl], preferred_element_type=F32)
        both += jnp.dot(slots_t[1], tok[other], preferred_element_type=F32)
        terms[h] = both.T.reshape(2, NY, WROWS, 2 * HDIM).astype(BF16)

    def rs_step(h, t):
        way = 1 if h % 2 == 0 else -1
        if t < 4:
            there = mod(y + way * (4 - t), NY)
            if t > 0:
                arrived(landed.at[h, t - 1], rs_recv.at[h, t - 1])
                terms[h, :, there] = (terms[h, :, there].astype(F32) + landed[h, t - 1].astype(F32)).astype(BF16)
            push(terms.at[h, :, there], landed.at[h, t], rs_send.at[h, t], rs_recv.at[h, t], at_y(way))
        if t < 3:
            there = mod(y - way * (3 - t), NY)
            if t > 0:
                arrived(landed.at[h, 3 + t], rs_recv.at[h, 3 + t])
                terms[h, :, there] = (terms[h, :, there].astype(F32) + landed[h, 3 + t].astype(F32)).astype(BF16)
            push(terms.at[h, :, there], landed.at[h, 4 + t], rs_send.at[h, 4 + t], rs_recv.at[h, 4 + t], at_y(-way))
        if t == 4:
            rs_end(h, (3, 6))

    def rs_end(h, last):
        whole = terms[h, :, y].astype(F32)
        for i in last:
            arrived(landed.at[h, i], rs_recv.at[h, i])
            whole += landed[h, i].astype(F32)
        total[h] = whole
        for i, out in enumerate((kg_out, vg_out)):
            there = out.at[0, :, own_columns(h)]
            half = pl.ds(i * HDIM, HDIM)
            push(total.at[h, other, :, half], there, fz_send.at[h, i], fz_recv.at[h, i], partner)
            copy = pltpu.make_async_copy(total.at[h, zl, :, half], there, fl_sem.at[h, i])
            copy.start()
            ends.append(copy)

    def rs_fast(h, stage_no):
        def on(step, i, ahead):
            there = terms.at[h, :, mod(y + ahead, NY)]
            push(there, landed.at[h, i], rs_send.at[h, i], rs_recv.at[h, i], at_y(step))

        if stage_no == 0:
            on(2, 0, 4)
            on(1, 1, 3)
            on(-1, 2, -3)
            on(1, 3, 1)
            on(-1, 4, -1)
        elif stage_no == 1:
            for ahead, got, i in ((-2, (2,), 6), (2, (1, 0), 5)):
                there = mod(y + ahead, NY)
                whole = terms[h, :, there].astype(F32)
                for j in got:
                    arrived(landed.at[h, j], rs_recv.at[h, j])
                    whole += landed[h, j].astype(F32)
                terms[h, :, there] = whole.astype(BF16)
                on(ahead, i, ahead)
        else:
            rs_end(h, (3, 4, 6, 5))

    def steps(*which):
        for f, h, t in which:
            f(h, t)

    w, g, f = w_step, rs_step, rs_fast
    after = [
        [(g, 0, 0), (w, 3, 2)],
        [(g, 1, 0), (g, 0, 1), (w, 3, 3)],
        [(f, 2, 0), (g, 1, 1), (g, 0, 2), (w, 3, 4)],
        [(f, 3, 0), (f, 2, 1), (g, 1, 2), (g, 0, 3), (f, 3, 1), (g, 1, 3), (g, 0, 4), (f, 2, 2), (g, 1, 4), (f, 3, 2)],
    ]
    w_slot(4)
    for h in range(HEADS):
        project(h)
        attend(h, 1)
        attend(h, 0)
        send_out(h)
        term(h)
        steps(*after[h])

    for h in range(HEADS):
        for i, (out, grad) in enumerate(((ctx_out, kg_out), (gq_out, vg_out))):
            arrived(out.at[0, :, other_columns(h)], oz_recv.at[h, i])
            arrived(grad.at[0, :, other_columns(h)], fz_recv.at[h, i])
    for copy in ends:
        copy.wait()
    for copy in sent:
        copy.wait_send()


def settle(*refs):
    ins, outs, bufs, sems = refs[:4], refs[4:8], refs[8:12], refs[12]
    inward = [pltpu.make_async_copy(a, b, sems.at[0, i]) for i, (a, b) in enumerate(zip(ins, bufs, strict=True))]
    outward = [pltpu.make_async_copy(a, b, sems.at[1, i]) for i, (a, b) in enumerate(zip(bufs, outs, strict=True))]
    for copy in inward:
        copy.start()
    for copy, later in zip(inward, outward, strict=True):
        copy.wait()
        later.start()
    for copy in outward:
        copy.wait()


def body(queries, grad_context, encodings, table, counts, key_weight, value_weight):
    any_ref = pl.BlockSpec(memory_space=pl.ANY)
    vmem = pl.BlockSpec(memory_space=pltpu.VMEM)
    smem = pl.BlockSpec(memory_space=pltpu.SMEM)
    dma = pltpu.SemaphoreType.DMA
    ring = dma((HEADS, 7))
    pair = dma((HEADS, 2))
    eight = dma((NZ,))
    local = key_weight.shape[2]
    scratch = [
        pltpu.VMEM((2, NZH, NX, 2, CHUNK, ENC), BF16),
        pltpu.VMEM((2, TOKENS, ENC), BF16),
        pltpu.VMEM((HEADS, 2, NY, WROWS, 2 * HDIM), BF16),
        pltpu.VMEM((2, HEADS, 2, ROWS, HDIM), BF16),
        pltpu.VMEM((2, 8, TOKENS), F32),
        pltpu.VMEM((2, BLOCKS, 8, TOKENS), F32),
        pltpu.VMEM((2, TOKENS, HDIM), BF16),
        pltpu.VMEM((2, TOKENS, HDIM), BF16),
        pltpu.VMEM((2, 2 * HDIM, TOKENS), BF16),
        pltpu.VMEM((HEADS, 2, NY, WROWS, 2 * HDIM), BF16),
        pltpu.VMEM((HEADS, 7, 2, WROWS, 2 * HDIM), BF16),
        pltpu.VMEM((2, HEADS, 2, ROWS, HDIM), BF16),
        pltpu.VMEM((HEADS, 2, WROWS, 2 * HDIM), F32),
        dma((2,)), eight, eight, eight, eight, eight, eight, eight, eight, dma((NZ * NX,)), dma((NZ * NX,)),
        pair, pair, pair, ring, ring, pair, pair, pair, ring, ring,
        pair, pair, pair, pair, pair, pair,
    ]
    outs = pl.pallas_call(
        kernel,
        out_shape=(
            jax.ShapeDtypeStruct((1, ROWS, local), BF16),
            jax.ShapeDtypeStruct((1, ROWS, local), BF16),
            jax.ShapeDtypeStruct((1, WROWS, local), F32),
            jax.ShapeDtypeStruct((1, WROWS, local), F32),
        ),
        in_specs=[vmem, smem, any_ref, any_ref, vmem, any_ref, any_ref],
        out_specs=(any_ref,) * 4,
        scratch_shapes=scratch,
        compiler_params=pltpu.CompilerParams(
            collective_id=0, has_side_effects=True, vmem_limit_bytes=56 * 1024 * 1024
        ),
    )(table.T, counts, queries, grad_context, encodings, key_weight, value_weight)
    return pl.pallas_call(
        settle,
        out_shape=tuple(jax.ShapeDtypeStruct(o.shape, o.dtype) for o in outs),
        in_specs=[any_ref] * 4,
        out_specs=(any_ref,) * 4,
        scratch_shapes=[*(pltpu.VMEM(o.shape, o.dtype) for o in outs), dma((2, 4))],
        compiler_params=pltpu.CompilerParams(vmem_limit_bytes=60 * 1024 * 1024),
    )(*outs)


def solution(mesh):
    in_specs = (
        P("section", "dp", "mp"),
        P("section", "dp", "mp"),
        P("dp", ("section", "mp"), None),
        P("dp", None),
        P("dp"),
        P("section", "dp", "mp"),
        P("section", "dp", "mp"),
    )
    out_specs = (
        P("section", "dp", "mp"),
        P("section", "dp", "mp"),
        P("section", "dp", "mp"),
        P("section", "dp", "mp"),
    )
    return jax.shard_map(body, mesh=mesh, in_specs=in_specs, out_specs=out_specs, check_vma=False)
```

```python
import functools

import jax
import jax.numpy as jnp
from jax import lax
from jax.experimental import pallas as pl
from jax.experimental.pallas import tpu as pltpu
from jax.sharding import PartitionSpec as P

MESH = pl.DeviceIdType.MESH
F32, BF16 = jnp.float32, jnp.bfloat16
HDIM = 128
LOG2E = 1.4426950408889634
NY, NX, NZH, NZ = 8, 4, 4, 8
HEADS = 4
SLOTS, PIECE, ENC = 6, 4, 896
CHUNK = SLOTS * PIECE
TOKENS = 768
ROWS, BLOCK, BLOCKS = 192, 64, 3
WROWS = 56
QL, QS, QR, MS, MR, WZ, WY, SS, SR, XS, OL, OS, OR, FL = range(14)
LATE = (3, 4, 5)


def mod(value, n):
    return lax.rem(value + n, n)


def kernel(
    table_ref, counts_ref, q_ref, g_ref, enc_ref, wk_ref, wv_ref,
    ctx_out, gq_out, kg_out, vg_out,
    ebuf, tok, wraw, qg, mult, times, keys, values, slots_t, terms, landed, stage, total,
    one_sem, z_send, z_recv, xp_recv, xm_recv, xo_recv, wl_sem, wz_recv, wy_recv, rs_send, rs_recv,
):
    dp, section, zh = lax.axis_index("dp"), lax.axis_index("section"), lax.axis_index("mp")
    zl, y = dp // NY, lax.rem(dp, NY)
    x, core = section // 2, lax.rem(section, 2)
    z = zh * 2 + zl
    other = 1 - zl

    partner = {"dp": other * NY + y}
    sibling = {"section": x * 2 + 1 - core}

    def at_y(step):
        return {"dp": zl * NY + mod(y + step, NY)}

    def across(step):
        return {"dp": other * NY + mod(y + step, NY)}

    def at_x(step):
        return {"section": mod(x + step, NX) * 2 + core}

    def at_z(step):
        there = mod(z + step, NZ)
        return {"dp": lax.rem(there, 2) * NY + y, "mp": there // 2}

    def remote(src, dst, send, recv, device):
        return pltpu.make_async_remote_copy(
            src_ref=src, dst_ref=dst, send_sem=send, recv_sem=recv, device_id=device, device_id_type=MESH
        )

    def push(src, dst, send, recv, device):
        remote(src, dst, send, recv, device).start()

    def arrived(ref, recv):
        remote(ref, ref, recv, recv, sibling).wait_recv()

    def left(ref, send):
        remote(ref, ref, send, send, sibling).wait_send()

    def moved(ref, sem):
        pltpu.make_async_copy(ref, ref, sem).wait()

    barrier = pltpu.get_barrier_semaphore()
    friends = [at_z(d) for d in (1, -1, 2, -2)] + [at_x(d) for d in (1, -1, 2)] + [sibling]
    friends += [at_y(d) for d in (1, -1, 2, -2)] + [across(d) for d in (1, -1, 2, -2)]
    for friend in friends:
        pl.semaphore_signal(barrier, inc=1, device_id=friend, device_id_type=MESH)

    def own_columns(h):
        return pl.ds(pl.multiple_of(zl * HEADS * HDIM + h * HDIM, HDIM), HDIM)

    def other_columns(h):
        return pl.ds(pl.multiple_of(other * HEADS * HDIM + h * HDIM, HDIM), HDIM)

    for h in range(HEADS):
        for i, w_ref in enumerate((wk_ref, wv_ref)):
            there = wraw.at[h, zl, y, :, pl.ds(i * HDIM, HDIM)]
            pltpu.make_async_copy(w_ref.at[0, :, own_columns(h)], there, wl_sem.at[h // 2]).start()
    for h in range(HEADS):
        for i, w_ref in enumerate((q_ref, g_ref)):
            pltpu.make_async_copy(w_ref.at[0, :, own_columns(h)], qg.at[0, h, i], one_sem.at[QL]).start()
    pieces = [enc_ref[s].astype(F32) for s in range(SLOTS)]
    ebuf[zl, zh, x, core] = jnp.concatenate(pieces, axis=0).astype(BF16)
    token = lax.broadcasted_iota(jnp.int32, (8, TOKENS), 1)
    slot_of = (token - CHUNK * ((token * 2731) >> 16)) >> 2
    row = lax.broadcasted_iota(jnp.int32, (8, TOKENS), 0)
    compact = jnp.zeros((8, TOKENS), F32)
    for c in range(BLOCKS):
        first = jnp.where(slot_of == table_ref[pl.ds(0, 1), pl.ds(c, 1)], 1.0, 0.0)
        second = jnp.where(slot_of == table_ref[pl.ds(1, 1), pl.ds(c, 1)], 1.0, 0.0)
        both = first + second * jnp.where(counts_ref[c] > 1, 1.0, 0.0)
        compact = jnp.where(row == c, both, compact)
    mult[0] = compact

    pl.semaphore_wait(barrier, len(friends))

    def chunk(dz, dx, core_of):
        zz = mod(z + dz, NZ)
        return ebuf.at[lax.rem(zz, 2), zz // 2, mod(x + dx, NX), core_of]

    mine = chunk(0, 0, core)
    for d in (1, 7, 2, 6):
        push(mine, mine, z_send.at[d], z_recv.at[d], at_z(d if d < 4 else d - NZ))

    def send_weights():
        for h in range(HEADS):
            for i, w_ref in enumerate((wk_ref, wv_ref)):
                push(
                    w_ref.at[0, :, other_columns(h)], wraw.at[h, zl, y, :, pl.ds(i * HDIM, HDIM)],
                    one_sem.at[WZ], wz_recv.at[h // 2], partner,
                )

    def send_rows():
        push(mult.at[0], mult.at[1], one_sem.at[MS], one_sem.at[MR], partner)
        for h in range(HEADS):
            for i, w_ref in enumerate((q_ref, g_ref)):
                push(w_ref.at[0, :, other_columns(h)], qg.at[1, h, i], one_sem.at[QS], one_sem.at[QR], partner)

    def w_step(pair, half, t):
        way = -1 if half else 1
        whose = other if half else zl

        def block(back):
            return wraw.at[pl.ds(2 * pair, 2), whose, mod(y - back, NY)]

        def on(back, step, i):
            push(block(back), block(back), one_sem.at[WY], wy_recv.at[pair, half, i], at_y(step))

        if t == 0:
            if half:
                arrived(block(0), wz_recv.at[pair])
            else:
                moved(block(0), wl_sem.at[pair])
        else:
            arrived(block(way * t), wy_recv.at[pair, half, t - 1])
        if t < 4:
            on(way * t, way, t)
        if 0 < t < 4:
            arrived(block(-way * t), wy_recv.at[pair, half, 3 + t])
        if t < 3:
            on(-way * t, -way, 4 + t)

    def to_sibling(ref):
        push(ref, ref, one_sem.at[SS], one_sem.at[SR], sibling)

    def e_first(d):
        ref = chunk(-d, 0, core)
        if d:
            arrived(ref, z_recv.at[d])
        if d == 2:
            push(ref, ref, z_send.at[4], z_recv.at[4], at_z(2))
            push(ref, ref, z_send.at[3], z_recv.at[3], at_z(1))
        if d == 6:
            push(ref, ref, z_send.at[5], z_recv.at[5], at_z(-1))
        push(ref, ref, one_sem.at[XS], xp_recv.at[d], at_x(1))
        push(ref, ref, one_sem.at[XS], xm_recv.at[d], at_x(-1))
        if d in LATE:
            push(ref, ref, one_sem.at[XS], xo_recv.at[d], at_x(2))
        to_sibling(ref)

    def e_second(d):
        ref = chunk(-d, -1, core)
        arrived(ref, xp_recv.at[d])
        if d % 2 == 0 and d not in LATE:
            push(ref, ref, one_sem.at[XS], xo_recv.at[d], at_x(1))
        to_sibling(ref)
        ref = chunk(-d, 1, core)
        arrived(ref, xm_recv.at[d])
        if d % 2 == 1 and d not in LATE:
            push(ref, ref, one_sem.at[XS], xo_recv.at[d], at_x(-1))
        to_sibling(ref)

    def e_third(d):
        ref = chunk(-d, 2, core)
        arrived(ref, xo_recv.at[d])
        to_sibling(ref)

    def each(f, *offsets):
        for d in offsets:
            f(d)

    send_weights()
    w_step(0, 0, 0)
    e_first(0)
    each(e_first, 1, 7)
    w_step(0, 0, 1)
    w_step(0, 1, 0)
    e_second(0)
    each(e_first, 2, 6)
    w_step(1, 0, 0)
    w_step(0, 0, 2)
    w_step(0, 1, 1)
    each(e_second, 1, 7)
    e_third(0)
    each(e_first, 3, 5)
    w_step(1, 1, 0)
    e_first(4)
    send_rows()
    w_step(0, 0, 3)
    w_step(0, 1, 2)
    each(e_second, 2, 6)
    w_step(1, 0, 1)
    each(e_third, 1, 7)
    each(e_second, 3, 5)
    w_step(1, 1, 1)
    w_step(0, 1, 3)
    e_second(4)
    each(e_third, 2, 6)
    w_step(1, 0, 2)
    each(e_third, 3, 5, 4)
    w_step(1, 1, 2)
    w_step(0, 0, 4)
    w_step(0, 1, 4)
    arrived(ebuf.at[0], one_sem.at[SR])
    moved(qg.at[0], one_sem.at[QL])
    arrived(qg.at[1], one_sem.at[QR])
    arrived(mult.at[1], one_sem.at[MR])

    for near in range(2):
        for c in range(BLOCKS):
            times[near, c] = jnp.broadcast_to(mult[near, pl.ds(c, 1), :], (8, TOKENS))

    for r in range(2):

        @pl.loop(0, NZH)
        def _(zz):
            part = ebuf[r, zz].reshape(NX * 2, CHUNK, ENC).astype(F32).reshape(NX * 2 * CHUNK, ENC)
            span = pl.ds(pl.multiple_of(zz * NX * 2 * CHUNK, NX * 2 * CHUNK), NX * 2 * CHUNK)
            tok[r, span, :] = part.astype(BF16)

    scale = HDIM**-0.5

    def project(h):
        @pl.loop(0, 2)
        def _(r):
            kv = jnp.dot(tok[r], wraw[h].reshape(2 * NY * WROWS, 2 * HDIM), preferred_element_type=F32).astype(BF16)
            keys[r] = kv[:, :HDIM]
            values[r] = kv[:, HDIM:]

    def nt(a, b):
        return lax.dot_general(a, b, (((1,), (1,)), ((), ())), preferred_element_type=F32)

    def tn(a, b):
        return lax.dot_general(a, b, (((0,), (0,)), ((), ())), preferred_element_type=F32)

    def attend(h, near):
        r = zl if near == 0 else other
        k, v = keys[r], values[r]
        q, g = qg[near, h, 0], qg[near, h, 1]
        shape = (BLOCKS, BLOCK // 8, 8, TOKENS)
        m = times[near].reshape(BLOCKS, 1, 8, TOKENS)
        scores = nt(q, k).reshape(shape) + jnp.where(m > 0.0, 0.0, -1e30)
        top = jnp.max(scores, axis=3, keepdims=True)
        weights = jnp.exp2((scores - top) * (scale * LOG2E)) * m
        probs = weights * (1.0 / jnp.sum(weights, axis=3, keepdims=True))
        dprob = nt(g, v).reshape(shape)
        delta = jnp.sum(probs * dprob, axis=3, keepdims=True)
        s = (probs * ((dprob - delta) * scale)).reshape(ROWS, TOKENS).astype(BF16)
        p = probs.reshape(ROWS, TOKENS).astype(BF16)
        stage[near, h, 0] = jnp.dot(p, v, preferred_element_type=F32).astype(BF16)
        stage[near, h, 1] = jnp.dot(s, k, preferred_element_type=F32).astype(BF16)
        slots_t[near, pl.ds(0, HDIM), :] = tn(q, s).astype(BF16)
        slots_t[near, pl.ds(HDIM, HDIM), :] = tn(g, p).astype(BF16)

    def send_out(h):
        for i, out in enumerate((ctx_out, gq_out)):
            there = out.at[0, :, own_columns(h)]
            push(stage.at[1, h, i], there, one_sem.at[OS], one_sem.at[OR], partner)
            pltpu.make_async_copy(stage.at[0, h, i], there, one_sem.at[OL]).start()

    def term(h):
        both = jnp.dot(slots_t[0], tok[zl], preferred_element_type=F32)
        both += jnp.dot(slots_t[1], tok[other], preferred_element_type=F32)
        terms[h] = both.T.reshape(2, NY, WROWS, 2 * HDIM).astype(BF16)

    def reduce(h, stage_no):
        for half in range(2):
            way = -1 if half else 1
            whose = other if half else zl

            def on(step, i, ahead, half=half, way=way, whose=whose):
                there = terms.at[h, whose, mod(y + way * ahead, NY)]
                device = across(way * step) if half and i > 2 else at_y(way * step)
                push(there, landed.at[h, half, i], rs_send.at[half], rs_recv.at[h, half, i], device)

            if stage_no == 0:
                on(2, 0, 4)
                on(1, 1, 3)
                on(-1, 2, -3)
                on(1, 3, 1)
                on(-1, 4, -1)
                if half:
                    on(0, 7, 0)
            elif stage_no == 1:
                for ahead, got, i in ((-2, (2,), 6), (2, (1, 0), 5)):
                    there = mod(y + way * ahead, NY)
                    whole = terms[h, whose, there].astype(F32)
                    for j in got:
                        arrived(landed.at[h, half, j], rs_recv.at[h, half, j])
                        whole += landed[h, half, j].astype(F32)
                    terms[h, whose, there] = whole.astype(BF16)
                    on(ahead, i, ahead)
            else:
                last = (3, 4, 6, 5)
                if half:
                    arrived(landed.at[h, 1, 7], rs_recv.at[h, 1, 7])
                    whole = landed[h, 1, 7].astype(F32)
                else:
                    whole = terms[h, zl, y].astype(F32)
                for i in last:
                    arrived(landed.at[h, half, i], rs_recv.at[h, half, i])
                    whole += landed[h, half, i].astype(F32)
                total[h, half] = whole
                columns = other_columns(h) if half else own_columns(h)
                for i, out in enumerate((kg_out, vg_out)):
                    part = total.at[h, half, :, pl.ds(i * HDIM, HDIM)]
                    pltpu.make_async_copy(part, out.at[0, :, columns], one_sem.at[FL]).start()

    for h in range(HEADS):
        if h == 2:
            w_step(1, 0, 4)
            w_step(1, 1, 4)
        project(h)
        if h == 0:
            w_step(1, 0, 3)
            w_step(1, 1, 3)
        if h > 1:
            reduce(h - 2, 1)
        attend(h, 1)
        attend(h, 0)
        send_out(h)
        if h > 2:
            reduce(h - 3, 2)
        term(h)
        reduce(h, 0)
    reduce(HEADS - 2, 1)
    reduce(HEADS - 3, 2)
    reduce(HEADS - 1, 1)
    reduce(HEADS - 2, 2)
    reduce(HEADS - 1, 2)

    arrived(stage.at[1], one_sem.at[OR])
    moved(stage.at[0], one_sem.at[OL])
    moved(total, one_sem.at[FL])
    left(stage.at[1], one_sem.at[OS])
    left(mult.at[0], one_sem.at[MS])
    left(qg.at[1], one_sem.at[QS])
    left(wraw.at[:, 0, 0], one_sem.at[WZ])
    left(wraw.at[:, :, pl.ds(0, 7)], one_sem.at[WY])
    left(ebuf.at[0], one_sem.at[SS])
    left(ebuf.at[0, pl.ds(0, 3)], one_sem.at[XS])
    left(landed.at[:, 0, pl.ds(0, 7)], rs_send.at[0])
    left(landed.at[:, 1], rs_send.at[1])
    for d in range(1, NZ):
        left(chunk(0, 0, core), z_send.at[d])


def settle(*refs):
    ins, outs, bufs, sems = refs[:4], refs[4:8], refs[8:12], refs[12]
    inward = [pltpu.make_async_copy(a, b, sems.at[0, i]) for i, (a, b) in enumerate(zip(ins, bufs, strict=True))]
    outward = [pltpu.make_async_copy(a, b, sems.at[1, i]) for i, (a, b) in enumerate(zip(bufs, outs, strict=True))]
    for copy in inward:
        copy.start()
    for copy, later in zip(inward, outward, strict=True):
        copy.wait()
        later.start()
    for copy in outward:
        copy.wait()


def body(queries, grad_context, encodings, table, counts, key_weight, value_weight):
    any_ref = pl.BlockSpec(memory_space=pl.ANY)
    vmem = pl.BlockSpec(memory_space=pltpu.VMEM)
    smem = pl.BlockSpec(memory_space=pltpu.SMEM)
    dma = pltpu.SemaphoreType.DMA
    eight = dma((NZ,))
    local = key_weight.shape[2]
    scratch = [
        pltpu.VMEM((2, NZH, NX, 2, CHUNK, ENC), BF16),
        pltpu.VMEM((2, TOKENS, ENC), BF16),
        pltpu.VMEM((HEADS, 2, NY, WROWS, 2 * HDIM), BF16),
        pltpu.VMEM((2, HEADS, 2, ROWS, HDIM), BF16),
        pltpu.VMEM((2, 8, TOKENS), F32),
        pltpu.VMEM((2, BLOCKS, 8, TOKENS), F32),
        pltpu.VMEM((2, TOKENS, HDIM), BF16),
        pltpu.VMEM((2, TOKENS, HDIM), BF16),
        pltpu.VMEM((2, 2 * HDIM, TOKENS), BF16),
        pltpu.VMEM((HEADS, 2, NY, WROWS, 2 * HDIM), BF16),
        pltpu.VMEM((HEADS, 2, 8, WROWS, 2 * HDIM), BF16),
        pltpu.VMEM((2, HEADS, 2, ROWS, HDIM), BF16),
        pltpu.VMEM((HEADS, 2, WROWS, 2 * HDIM), F32),
        dma((14,)), eight, eight, eight, eight, eight, dma((2,)), dma((2,)), dma((2, 2, 7)), dma((2,)), dma((HEADS, 2, 8)),
    ]
    outs = pl.pallas_call(
        kernel,
        out_shape=(
            jax.ShapeDtypeStruct((1, ROWS, local), BF16),
            jax.ShapeDtypeStruct((1, ROWS, local), BF16),
            jax.ShapeDtypeStruct((1, WROWS, local), F32),
            jax.ShapeDtypeStruct((1, WROWS, local), F32),
        ),
        in_specs=[vmem, smem, any_ref, any_ref, vmem, any_ref, any_ref],
        out_specs=(any_ref,) * 4,
        scratch_shapes=scratch,
        compiler_params=pltpu.CompilerParams(
            collective_id=0, has_side_effects=True, vmem_limit_bytes=56 * 1024 * 1024
        ),
    )(table.T, counts, queries, grad_context, encodings, key_weight, value_weight)
    return pl.pallas_call(
        settle,
        out_shape=tuple(jax.ShapeDtypeStruct(o.shape, o.dtype) for o in outs),
        in_specs=[any_ref] * 4,
        out_specs=(any_ref,) * 4,
        scratch_shapes=[*(pltpu.VMEM(o.shape, o.dtype) for o in outs), dma((2, 4))],
        compiler_params=pltpu.CompilerParams(vmem_limit_bytes=60 * 1024 * 1024),
    )(*outs)


def solution(mesh):
    in_specs = (
        P("section", "dp", "mp"),
        P("section", "dp", "mp"),
        P("dp", ("section", "mp"), None),
        P("dp", None),
        P("dp"),
        P("section", "dp", "mp"),
        P("section", "dp", "mp"),
    )
    out_specs = (
        P("section", "dp", "mp"),
        P("section", "dp", "mp"),
        P("section", "dp", "mp"),
        P("section", "dp", "mp"),
    )
    return jax.shard_map(body, mesh=mesh, in_specs=in_specs, out_specs=out_specs, check_vma=False)
```

```python
import functools

import jax
import jax.numpy as jnp
from jax import lax
from jax.experimental import pallas as pl
from jax.experimental.pallas import tpu as pltpu
from jax.sharding import PartitionSpec as P

MESH = pl.DeviceIdType.MESH
F32, BF16 = jnp.float32, jnp.bfloat16
HDIM = 128
LOG2E = 1.4426950408889634
NY, NX, NZH, NZ = 8, 4, 4, 8
HEADS = 4
SLOTS, PIECE, ENC = 6, 4, 896
CHUNK = SLOTS * PIECE
TOKENS = 768
ROWS, BLOCK, BLOCKS = 192, 64, 3
WROWS = 56
GROUPS = ((0,), (1,), (2, 3))
GROUP_OF = (0, 1, 2, 2)
W_TWO = (((0, 2), (0, -2), (0, 1), (0, -1)), ((2, 4), (2, 3), (-2, -3)))
W_THREE = (((0, 1), (0, -1)), ((1, 3), (1, 2), (-1, -2)), ((3, 4), (-2, -3)))
W_PLANS = (W_TWO, W_TWO, W_THREE)
RING = (((4, 3), (-3, -2)), ((3, 2), (-2, -1)), ((2, 1), (-1, 0)), ((1, 0),))
THREE = (((4, 3), (2, 1), (-3, -2)), ((3, 1), (-2, -1)), ((1, 0), (-1, 0)))
TWO = (((4, 2), (3, 2), (-3, -2), (1, 0), (-1, 0)), ((2, 0), (-2, 0)))
PLANS = (RING, RING, THREE, TWO)
QL, QS, MS, MR, WZ, WY, SS, SR, XS, OL, OS, OR, FL, BX, BZ, BF = range(16)
FIRST = 640
LATE = (3, 4, 5)


def mod(value, n):
    return lax.rem(value + n, n)


def kernel(
    table_ref, counts_ref, q_ref, g_ref, enc_ref, wk_ref, wv_ref,
    ctx_out, gq_out, kg_out, vg_out,
    ebuf, tok, wraw, qg, mult, times, keys, values, slots_t, terms, landed, stage, total,
    one_sem, z_send, z_recv, xp_recv, xm_recv, xo_recv, bx_recv, bz_recv, qr_sem, wl_sem, wz_recv, wy_recv, rs_send, rs_recv,
):
    dp, section, zh = lax.axis_index("dp"), lax.axis_index("section"), lax.axis_index("mp")
    zl, y = dp // NY, lax.rem(dp, NY)
    x, core = section // 2, lax.rem(section, 2)
    z = zh * 2 + zl
    other = 1 - zl

    partner = {"dp": other * NY + y}
    sibling = {"section": x * 2 + 1 - core}

    def at_y(step):
        return {"dp": zl * NY + mod(y + step, NY)}

    def across(step):
        return {"dp": other * NY + mod(y + step, NY)}

    def at_x(step):
        return {"section": mod(x + step, NX) * 2 + core}

    def at_z(step):
        there = mod(z + step, NZ)
        return {"dp": lax.rem(there, 2) * NY + y, "mp": there // 2}

    def remote(src, dst, send, recv, device):
        return pltpu.make_async_remote_copy(
            src_ref=src, dst_ref=dst, send_sem=send, recv_sem=recv, device_id=device, device_id_type=MESH
        )

    def push(src, dst, send, recv, device):
        remote(src, dst, send, recv, device).start()

    def arrived(ref, recv):
        remote(ref, ref, recv, recv, sibling).wait_recv()

    def left(ref, send):
        remote(ref, ref, send, send, sibling).wait_send()

    def moved(ref, sem):
        pltpu.make_async_copy(ref, ref, sem).wait()

    barrier = pltpu.get_barrier_semaphore()
    friends = [at_z(d) for d in (1, -1, 2, -2)] + [at_x(d) for d in (1, -1, 2)] + [sibling]
    friends += [at_y(d) for d in (1, -1, 2, -2)] + [across(d) for d in (1, -1, 2, -2)]
    for friend in friends:
        pl.semaphore_signal(barrier, inc=1, device_id=friend, device_id_type=MESH)

    def own_columns(h):
        return pl.ds(pl.multiple_of(zl * HEADS * HDIM + h * HDIM, HDIM), HDIM)

    def other_columns(h):
        return pl.ds(pl.multiple_of(other * HEADS * HDIM + h * HDIM, HDIM), HDIM)

    for h in range(HEADS):
        for i, w_ref in enumerate((wk_ref, wv_ref)):
            there = wraw.at[h, zl, y, :, pl.ds(i * HDIM, HDIM)]
            pltpu.make_async_copy(w_ref.at[0, :, own_columns(h)], there, wl_sem.at[GROUP_OF[h]]).start()
    for h in range(HEADS):
        for i, w_ref in enumerate((q_ref, g_ref)):
            pltpu.make_async_copy(w_ref.at[0, :, own_columns(h)], qg.at[0, h, i], one_sem.at[QL]).start()
    pieces = [enc_ref[s].astype(F32) for s in range(SLOTS)]
    ebuf[zl, zh, x, core] = jnp.concatenate(pieces, axis=0).astype(BF16)
    token = lax.broadcasted_iota(jnp.int32, (8, TOKENS), 1)
    slot_of = (token - CHUNK * ((token * 2731) >> 16)) >> 2
    row = lax.broadcasted_iota(jnp.int32, (8, TOKENS), 0)
    compact = jnp.zeros((8, TOKENS), F32)
    for c in range(BLOCKS):
        first = jnp.where(slot_of == table_ref[pl.ds(0, 1), pl.ds(c, 1)], 1.0, 0.0)
        second = jnp.where(slot_of == table_ref[pl.ds(1, 1), pl.ds(c, 1)], 1.0, 0.0)
        both = first + second * jnp.where(counts_ref[c] > 1, 1.0, 0.0)
        compact = jnp.where(row == c, both, compact)
    mult[0] = compact

    pl.semaphore_wait(barrier, len(friends))

    def chunk(dz, dx, core_of):
        zz = mod(z + dz, NZ)
        return ebuf.at[lax.rem(zz, 2), zz // 2, mod(x + dx, NX), core_of, :, pl.ds(0, FIRST)]

    rest = pl.ds(FIRST, ENC - FIRST)

    def tail_of(dx):
        return ebuf.at[zl, zh, mod(x + dx, NX), core, :, rest]

    def tails(dz):
        zz = mod(z + dz, NZ)
        return ebuf.at[lax.rem(zz, 2), zz // 2, :, core, :, rest]

    mine = chunk(0, 0, core)

    def send_chunk():
        for d in (1, 7, 2, 6):
            push(mine, mine, z_send.at[d], z_recv.at[d], at_z(d if d < 4 else d - NZ))

    def send_tail():
        for dx in (1, -1, 2):
            push(tail_of(0), tail_of(0), one_sem.at[BX], bx_recv.at[dx % NX], at_x(dx))

    def tail_first():
        for dx in (1, 2, 3):
            arrived(tail_of(-dx), bx_recv.at[dx])
        for d in (2, 6, 1, 7):
            push(tails(0), tails(0), one_sem.at[BZ], bz_recv.at[d], at_z(d if d < 4 else d - NZ))
        to_sibling(tails(0))

    def tail_second():
        arrived(tails(-2), bz_recv.at[2])
        push(tails(-2), tails(-2), one_sem.at[BF], bz_recv.at[4], at_z(2))
        push(tails(-2), tails(-2), one_sem.at[BF], bz_recv.at[3], at_z(1))
        arrived(tails(2), bz_recv.at[6])
        push(tails(2), tails(2), one_sem.at[BF], bz_recv.at[5], at_z(-1))
        for d in (2, 6):
            to_sibling(tails(-d))

    def tail_third(*which):
        for d in which:
            arrived(tails(-d), bz_recv.at[d])
            to_sibling(tails(-d))

    def send_weights(group):
        for h in GROUPS[group]:
            for i, w_ref in enumerate((wk_ref, wv_ref)):
                push(
                    w_ref.at[0, :, other_columns(h)], wraw.at[h, zl, y, :, pl.ds(i * HDIM, HDIM)],
                    one_sem.at[WZ], wz_recv.at[group], partner,
                )

    def send_rows(h):
        for i, w_ref in enumerate((q_ref, g_ref)):
            push(w_ref.at[0, :, other_columns(h)], qg.at[1, h, i], one_sem.at[QS], qr_sem.at[h], partner)

    here = set()

    def w_step(group, half, t):
        heads, plan = GROUPS[group], W_PLANS[group]
        edges = [edge for round_ in plan for edge in round_]
        way = -1 if half else 1
        whose = other if half else zl

        def block(a):
            return wraw.at[pl.ds(heads[0], len(heads)), whose, mod(y - way * a, NY)]

        def need(a):
            if (group, half, a) not in here:
                here.add((group, half, a))
                if a:
                    i = [edge[1] for edge in edges].index(a)
                    arrived(block(a), wy_recv.at[group, half, i])
                elif half:
                    arrived(block(0), wz_recv.at[group])
                else:
                    moved(block(0), wl_sem.at[group])

        if t < len(plan):
            for a, b in plan[t]:
                need(a)
                there = wy_recv.at[group, half, edges.index((a, b))]
                push(block(a), block(a), one_sem.at[WY], there, at_y(way * (b - a)))
        else:
            for _, b in edges:
                need(b)

    def to_sibling(ref):
        push(ref, ref, one_sem.at[SS], one_sem.at[SR], sibling)

    def e_first(d):
        ref = chunk(-d, 0, core)
        if d:
            arrived(ref, z_recv.at[d])
        if d == 2:
            push(ref, ref, z_send.at[4], z_recv.at[4], at_z(2))
            push(ref, ref, z_send.at[3], z_recv.at[3], at_z(1))
        if d == 6:
            push(ref, ref, z_send.at[5], z_recv.at[5], at_z(-1))
        push(ref, ref, one_sem.at[XS], xp_recv.at[d], at_x(1))
        push(ref, ref, one_sem.at[XS], xm_recv.at[d], at_x(-1))
        if d in LATE:
            push(ref, ref, one_sem.at[XS], xo_recv.at[d], at_x(2))
        to_sibling(ref)

    def e_second(d):
        ref = chunk(-d, -1, core)
        arrived(ref, xp_recv.at[d])
        if d % 2 == 0 and d not in LATE:
            push(ref, ref, one_sem.at[XS], xo_recv.at[d], at_x(1))
        to_sibling(ref)
        ref = chunk(-d, 1, core)
        arrived(ref, xm_recv.at[d])
        if d % 2 == 1 and d not in LATE:
            push(ref, ref, one_sem.at[XS], xo_recv.at[d], at_x(-1))
        to_sibling(ref)

    def e_third(d):
        ref = chunk(-d, 2, core)
        arrived(ref, xo_recv.at[d])
        to_sibling(ref)

    def each(f, *offsets):
        for d in offsets:
            f(d)

    def weights(*which):
        for group, half, t in which:
            w_step(group, half, t)

    send_weights(0)
    send_tail()
    send_chunk()
    send_weights(1)
    weights((0, 0, 0), (1, 0, 0), (2, 0, 0))
    e_first(0)
    tail_first()
    each(e_first, 1, 7)
    w_step(0, 1, 0)
    each(e_first, 2, 6)
    send_weights(2)
    w_step(0, 0, 1)
    each(e_second, 0, 1, 7)
    weights((1, 1, 0), (1, 0, 1))
    tail_second()
    send_rows(0)
    push(mult.at[0], mult.at[1], one_sem.at[MS], one_sem.at[MR], partner)
    each(e_third, 0)
    each(e_first, 3, 5, 4)
    each(e_second, 2, 6)
    weights((0, 1, 1), (2, 1, 0), (2, 0, 1))
    tail_third(1, 7)
    each(e_third, 1, 7)
    each(e_second, 3, 5)
    weights((1, 1, 1), (0, 0, 2))
    tail_third(3, 5, 4)
    for h in range(1, HEADS):
        send_rows(h)
    each(e_third, 2, 6)
    e_second(4)
    each(e_third, 3, 5, 4)
    weights((2, 1, 1), (0, 1, 2))
    arrived(ebuf.at[0], one_sem.at[SR])
    moved(qg.at[0], one_sem.at[QL])
    arrived(mult.at[1], one_sem.at[MR])

    for near in range(2):
        for c in range(BLOCKS):
            times[near, c] = jnp.broadcast_to(mult[near, pl.ds(c, 1), :], (8, TOKENS))

    for r in range(2):

        @pl.loop(0, NZH)
        def _(zz):
            part = ebuf[r, zz].reshape(NX * 2, CHUNK, ENC).astype(F32).reshape(NX * 2 * CHUNK, ENC)
            span = pl.ds(pl.multiple_of(zz * NX * 2 * CHUNK, NX * 2 * CHUNK), NX * 2 * CHUNK)
            tok[r, span, :] = part.astype(BF16)

    scale = HDIM**-0.5

    def project(h):
        @pl.loop(0, 2)
        def _(r):
            kv = jnp.dot(tok[r], wraw[h].reshape(2 * NY * WROWS, 2 * HDIM), preferred_element_type=F32).astype(BF16)
            keys[r] = kv[:, :HDIM]
            values[r] = kv[:, HDIM:]

    def nt(a, b):
        return lax.dot_general(a, b, (((1,), (1,)), ((), ())), preferred_element_type=F32)

    def tn(a, b):
        return lax.dot_general(a, b, (((0,), (0,)), ((), ())), preferred_element_type=F32)

    def attend_one(h, near):
        r = zl if near == 0 else other
        k, v = keys[r], values[r]
        q, g = qg[near, h, 0], qg[near, h, 1]
        shape = (BLOCKS, BLOCK // 8, 8, TOKENS)
        m = times[near].reshape(BLOCKS, 1, 8, TOKENS)
        scores = nt(q, k).reshape(shape) + jnp.where(m > 0.0, 0.0, -1e30)
        top = jnp.max(scores, axis=3, keepdims=True)
        weights = jnp.exp2((scores - top) * (scale * LOG2E)) * m
        probs = weights * (1.0 / jnp.sum(weights, axis=3, keepdims=True))
        dprob = nt(g, v).reshape(shape)
        delta = jnp.sum(probs * dprob, axis=3, keepdims=True)
        s = (probs * ((dprob - delta) * scale)).reshape(ROWS, TOKENS).astype(BF16)
        p = probs.reshape(ROWS, TOKENS).astype(BF16)
        stage[near, h, 0] = jnp.dot(p, v, preferred_element_type=F32).astype(BF16)
        stage[near, h, 1] = jnp.dot(s, k, preferred_element_type=F32).astype(BF16)
        slots_t[near, pl.ds(0, HDIM), :] = tn(q, s).astype(BF16)
        slots_t[near, pl.ds(HDIM, HDIM), :] = tn(g, p).astype(BF16)

    def attend(h):
        arrived(qg.at[1, h], qr_sem.at[h])
        attend_one(h, 1)
        attend_one(h, 0)
        for i, out in enumerate((ctx_out, gq_out)):
            there = out.at[0, :, own_columns(h)]
            push(stage.at[1, h, i], there, one_sem.at[OS], one_sem.at[OR], partner)
            pltpu.make_async_copy(stage.at[0, h, i], there, one_sem.at[OL]).start()

    def term(h):
        both = jnp.dot(slots_t[0], tok[zl], preferred_element_type=F32)
        both += jnp.dot(slots_t[1], tok[other], preferred_element_type=F32)
        terms[h] = both.T.reshape(2, NY, WROWS, 2 * HDIM).astype(BF16)

    def reduce(h, stage_no):
        plan = PLANS[h]
        edges = [edge for round_ in plan for edge in round_]
        for half in range(2):
            way = -1 if half else 1
            whose = other if half else zl

            def gather(whole, b, h=h, half=half, edges=edges):
                for i, edge in enumerate(edges):
                    if edge[1] == b:
                        arrived(landed.at[h, half, i], rs_recv.at[h, half, i])
                        whole += landed[h, half, i].astype(F32)
                return whole

            if stage_no < len(plan):
                for a, b in plan[stage_no]:
                    i = edges.index((a, b))
                    there = mod(y + way * a, NY)
                    if any(edge[1] == a for edge in edges):
                        terms[h, whose, there] = gather(terms[h, whose, there].astype(F32), a).astype(BF16)
                    device = across(way * a) if half and b == 0 else at_y(way * (a - b))
                    push(terms.at[h, whose, there], landed.at[h, half, i], rs_send.at[half], rs_recv.at[h, half, i], device)
                if half and stage_no == 0:
                    push(terms.at[h, other, y], landed.at[h, 1, 7], rs_send.at[1], rs_recv.at[h, 1, 7], partner)
            else:
                if half:
                    arrived(landed.at[h, 1, 7], rs_recv.at[h, 1, 7])
                    whole = landed[h, 1, 7].astype(F32)
                else:
                    whole = terms[h, zl, y].astype(F32)
                total[h, half] = gather(whole, 0)
                columns = other_columns(h) if half else own_columns(h)
                for i, out in enumerate((kg_out, vg_out)):
                    part = total.at[h, half, :, pl.ds(i * HDIM, HDIM)]
                    pltpu.make_async_copy(part, out.at[0, :, columns], one_sem.at[FL]).start()

    def sums(*which):
        for h, stage_no in which:
            reduce(h, stage_no)

    project(0)
    w_step(2, 0, 2)
    attend(0)
    w_step(2, 1, 2)
    term(0)
    reduce(0, 0)
    weights((1, 0, 2), (1, 1, 2))
    project(1)
    attend(1)
    reduce(0, 1)
    term(1)
    reduce(1, 0)
    weights((2, 0, 3), (2, 1, 3))
    project(2)
    reduce(0, 2)
    attend(2)
    reduce(1, 1)
    term(2)
    reduce(2, 0)
    reduce(0, 3)
    project(3)
    reduce(1, 2)
    attend(3)
    term(3)
    sums((3, 0), (2, 1), (1, 3), (0, 4), (3, 1), (2, 2), (1, 4), (3, 2), (2, 3))

    arrived(stage.at[1], one_sem.at[OR])
    moved(stage.at[0], one_sem.at[OL])
    moved(total, one_sem.at[FL])
    left(stage.at[1], one_sem.at[OS])
    left(mult.at[0], one_sem.at[MS])
    left(qg.at[1], one_sem.at[QS])
    left(wraw.at[:, 0, 0], one_sem.at[WZ])
    left(wraw.at[:, :, pl.ds(0, 7)], one_sem.at[WY])
    left(ebuf.at[0], one_sem.at[SS])
    left(ebuf.at[0, pl.ds(0, 3), :, :, :, pl.ds(0, FIRST)], one_sem.at[XS])
    left(ebuf.at[0, 0, pl.ds(0, 3), 0, :, rest], one_sem.at[BX])
    left(ebuf.at[0, :, :, 0, :, rest], one_sem.at[BZ])
    left(ebuf.at[0, pl.ds(0, 3), :, 0, :, rest], one_sem.at[BF])
    left(landed.at[:, 0, pl.ds(0, 7)], rs_send.at[0])
    left(landed.at[:, 1], rs_send.at[1])
    for d in range(1, NZ):
        left(chunk(0, 0, core), z_send.at[d])


def settle(*refs):
    ins, outs, bufs, sems = refs[:4], refs[4:8], refs[8:12], refs[12]
    inward = [pltpu.make_async_copy(a, b, sems.at[0, i]) for i, (a, b) in enumerate(zip(ins, bufs, strict=True))]
    outward = [pltpu.make_async_copy(a, b, sems.at[1, i]) for i, (a, b) in enumerate(zip(bufs, outs, strict=True))]
    for copy in inward:
        copy.start()
    for copy, later in zip(inward, outward, strict=True):
        copy.wait()
        later.start()
    for copy in outward:
        copy.wait()


def body(queries, grad_context, encodings, table, counts, key_weight, value_weight):
    any_ref = pl.BlockSpec(memory_space=pl.ANY)
    vmem = pl.BlockSpec(memory_space=pltpu.VMEM)
    smem = pl.BlockSpec(memory_space=pltpu.SMEM)
    dma = pltpu.SemaphoreType.DMA
    eight = dma((NZ,))
    local = key_weight.shape[2]
    scratch = [
        pltpu.VMEM((2, NZH, NX, 2, CHUNK, ENC), BF16),
        pltpu.VMEM((2, TOKENS, ENC), BF16),
        pltpu.VMEM((HEADS, 2, NY, WROWS, 2 * HDIM), BF16),
        pltpu.VMEM((2, HEADS, 2, ROWS, HDIM), BF16),
        pltpu.VMEM((2, 8, TOKENS), F32),
        pltpu.VMEM((2, BLOCKS, 8, TOKENS), F32),
        pltpu.VMEM((2, TOKENS, HDIM), BF16),
        pltpu.VMEM((2, TOKENS, HDIM), BF16),
        pltpu.VMEM((2, 2 * HDIM, TOKENS), BF16),
        pltpu.VMEM((HEADS, 2, NY, WROWS, 2 * HDIM), BF16),
        pltpu.VMEM((HEADS, 2, 8, WROWS, 2 * HDIM), BF16),
        pltpu.VMEM((2, HEADS, 2, ROWS, HDIM), BF16),
        pltpu.VMEM((HEADS, 2, WROWS, 2 * HDIM), F32),
        dma((16,)), eight, eight, eight, eight, eight, dma((NX,)), eight, dma((HEADS,)), dma((3,)), dma((3,)), dma((3, 2, 7)), dma((2,)),
        dma((HEADS, 2, 8)),
    ]
    outs = pl.pallas_call(
        kernel,
        out_shape=(
            jax.ShapeDtypeStruct((1, ROWS, local), BF16),
            jax.ShapeDtypeStruct((1, ROWS, local), BF16),
            jax.ShapeDtypeStruct((1, WROWS, local), F32),
            jax.ShapeDtypeStruct((1, WROWS, local), F32),
        ),
        in_specs=[vmem, smem, any_ref, any_ref, vmem, any_ref, any_ref],
        out_specs=(any_ref,) * 4,
        scratch_shapes=scratch,
        compiler_params=pltpu.CompilerParams(
            collective_id=0, has_side_effects=True, vmem_limit_bytes=56 * 1024 * 1024
        ),
    )(table.T, counts, queries, grad_context, encodings, key_weight, value_weight)
    return pl.pallas_call(
        settle,
        out_shape=tuple(jax.ShapeDtypeStruct(o.shape, o.dtype) for o in outs),
        in_specs=[any_ref] * 4,
        out_specs=(any_ref,) * 4,
        scratch_shapes=[*(pltpu.VMEM(o.shape, o.dtype) for o in outs), dma((2, 4))],
        compiler_params=pltpu.CompilerParams(vmem_limit_bytes=60 * 1024 * 1024),
    )(*outs)


def solution(mesh):
    in_specs = (
        P("section", "dp", "mp"),
        P("section", "dp", "mp"),
        P("dp", ("section", "mp"), None),
        P("dp", None),
        P("dp"),
        P("section", "dp", "mp"),
        P("section", "dp", "mp"),
    )
    out_specs = (
        P("section", "dp", "mp"),
        P("section", "dp", "mp"),
        P("section", "dp", "mp"),
        P("section", "dp", "mp"),
    )
    return jax.shard_map(body, mesh=mesh, in_specs=in_specs, out_specs=out_specs, check_vma=False)
```

```python
import functools

import jax
import jax.numpy as jnp
from jax import lax
from jax.experimental import pallas as pl
from jax.experimental.pallas import tpu as pltpu
from jax.sharding import PartitionSpec as P

MESH = pl.DeviceIdType.MESH
F32, BF16 = jnp.float32, jnp.bfloat16
HDIM = 128
LOG2E = 1.4426950408889634
NY, NX, NZH, NZ = 8, 4, 4, 8
HEADS = 4
SLOTS, PIECE, ENC = 6, 4, 896
CHUNK = SLOTS * PIECE
TOKENS = 768
ROWS, BLOCK, BLOCKS = 192, 64, 3
WROWS = 56
GROUPS = ((0,), (1,), (2, 3))
GROUP_OF = (0, 1, 2, 2)
W_TWO = (((0, 2), (0, -2), (0, 1), (0, -1)), ((2, 4), (2, 3), (-2, -3)))
W_THREE = (((0, 1), (0, -1)), ((1, 3), (1, 2), (-1, -2)), ((3, 4), (-2, -3)))
W_PLANS = (W_TWO, W_TWO, W_THREE)
RING = (((4, 3), (-3, -2)), ((3, 2), (-2, -1)), ((2, 1), (-1, 0)), ((1, 0),))
TWO = (((4, 2), (3, 2), (-3, -2), (1, 0), (-1, 0)), ((2, 0), (-2, 0)))
PLANS = (RING, RING, TWO, TWO)
QL, QS, MS, MR, WZ, WY, SS, SR, XS, OL, OS, OR, FL, BX, BZ, BF = range(16)
FIRST = 640
LATE = (3, 4, 5)


def mod(value, n):
    return lax.rem(value + n, n)


def kernel(
    table_ref, counts_ref, q_ref, g_ref, enc_ref, wk_ref, wv_ref,
    ctx_out, gq_out, kg_out, vg_out,
    ebuf, tok, wraw, qg, mult, times, keys, values, slots_t, terms, landed, stage, total,
    one_sem, z_send, z_recv, xp_recv, xm_recv, xo_recv, bx_recv, bz_recv, qr_sem, wl_sem, wz_recv, wy_recv, rs_send, rs_recv,
):
    dp, section, zh = lax.axis_index("dp"), lax.axis_index("section"), lax.axis_index("mp")
    zl, y = dp // NY, lax.rem(dp, NY)
    x, core = section // 2, lax.rem(section, 2)
    z = zh * 2 + zl
    other = 1 - zl

    partner = {"dp": other * NY + y}
    sibling = {"section": x * 2 + 1 - core}

    def at_y(step):
        return {"dp": zl * NY + mod(y + step, NY)}

    def across(step):
        return {"dp": other * NY + mod(y + step, NY)}

    def at_x(step):
        return {"section": mod(x + step, NX) * 2 + core}

    def at_z(step):
        there = mod(z + step, NZ)
        return {"dp": lax.rem(there, 2) * NY + y, "mp": there // 2}

    def remote(src, dst, send, recv, device):
        return pltpu.make_async_remote_copy(
            src_ref=src, dst_ref=dst, send_sem=send, recv_sem=recv, device_id=device, device_id_type=MESH
        )

    def push(src, dst, send, recv, device):
        remote(src, dst, send, recv, device).start()

    def arrived(ref, recv):
        remote(ref, ref, recv, recv, sibling).wait_recv()

    def left(ref, send):
        remote(ref, ref, send, send, sibling).wait_send()

    def moved(ref, sem):
        pltpu.make_async_copy(ref, ref, sem).wait()

    barrier = pltpu.get_barrier_semaphore()
    friends = [at_z(d) for d in (1, -1, 2, -2)] + [at_x(d) for d in (1, -1, 2)] + [sibling]
    friends += [at_y(d) for d in (1, -1, 2, -2)] + [across(d) for d in (1, -1, 2, -2)]
    for friend in friends:
        pl.semaphore_signal(barrier, inc=1, device_id=friend, device_id_type=MESH)

    def own_columns(h):
        return pl.ds(pl.multiple_of(zl * HEADS * HDIM + h * HDIM, HDIM), HDIM)

    def other_columns(h):
        return pl.ds(pl.multiple_of(other * HEADS * HDIM + h * HDIM, HDIM), HDIM)

    for h in range(HEADS):
        for i, w_ref in enumerate((wk_ref, wv_ref)):
            there = wraw.at[h, zl, y, :, pl.ds(i * HDIM, HDIM)]
            pltpu.make_async_copy(w_ref.at[0, :, own_columns(h)], there, wl_sem.at[GROUP_OF[h]]).start()
    for h in range(HEADS):
        for i, w_ref in enumerate((q_ref, g_ref)):
            pltpu.make_async_copy(w_ref.at[0, :, own_columns(h)], qg.at[0, h, i], one_sem.at[QL]).start()
    pieces = [enc_ref[s].astype(F32) for s in range(SLOTS)]
    ebuf[zl, zh, x, core] = jnp.concatenate(pieces, axis=0).astype(BF16)
    token = lax.broadcasted_iota(jnp.int32, (8, TOKENS), 1)
    slot_of = (token - CHUNK * ((token * 2731) >> 16)) >> 2
    row = lax.broadcasted_iota(jnp.int32, (8, TOKENS), 0)
    compact = jnp.zeros((8, TOKENS), F32)
    for c in range(BLOCKS):
        first = jnp.where(slot_of == table_ref[pl.ds(0, 1), pl.ds(c, 1)], 1.0, 0.0)
        second = jnp.where(slot_of == table_ref[pl.ds(1, 1), pl.ds(c, 1)], 1.0, 0.0)
        both = first + second * jnp.where(counts_ref[c] > 1, 1.0, 0.0)
        compact = jnp.where(row == c, both, compact)
    mult[0] = compact

    pl.semaphore_wait(barrier, len(friends))

    def chunk(dz, dx, core_of):
        zz = mod(z + dz, NZ)
        return ebuf.at[lax.rem(zz, 2), zz // 2, mod(x + dx, NX), core_of, :, pl.ds(0, FIRST)]

    rest = pl.ds(FIRST, ENC - FIRST)

    def tail_of(dx):
        return ebuf.at[zl, zh, mod(x + dx, NX), core, :, rest]

    def tails(dz):
        zz = mod(z + dz, NZ)
        return ebuf.at[lax.rem(zz, 2), zz // 2, :, core, :, rest]

    mine = chunk(0, 0, core)

    def send_chunk():
        for d in (1, 7, 2, 6):
            push(mine, mine, z_send.at[d], z_recv.at[d], at_z(d if d < 4 else d - NZ))

    def send_tail():
        for dx in (1, -1, 2):
            push(tail_of(0), tail_of(0), one_sem.at[BX], bx_recv.at[dx % NX], at_x(dx))

    def tail_first():
        for dx in (1, 2, 3):
            arrived(tail_of(-dx), bx_recv.at[dx])
        for d in (2, 6, 1, 7):
            push(tails(0), tails(0), one_sem.at[BZ], bz_recv.at[d], at_z(d if d < 4 else d - NZ))
        to_sibling(tails(0))

    def tail_second():
        arrived(tails(-2), bz_recv.at[2])
        push(tails(-2), tails(-2), one_sem.at[BF], bz_recv.at[4], at_z(2))
        push(tails(-2), tails(-2), one_sem.at[BF], bz_recv.at[3], at_z(1))
        arrived(tails(2), bz_recv.at[6])
        push(tails(2), tails(2), one_sem.at[BF], bz_recv.at[5], at_z(-1))
        for d in (2, 6):
            to_sibling(tails(-d))

    def tail_third(*which):
        for d in which:
            arrived(tails(-d), bz_recv.at[d])
            to_sibling(tails(-d))

    def send_weights(group):
        for h in GROUPS[group]:
            for i, w_ref in enumerate((wk_ref, wv_ref)):
                push(
                    w_ref.at[0, :, other_columns(h)], wraw.at[h, zl, y, :, pl.ds(i * HDIM, HDIM)],
                    one_sem.at[WZ], wz_recv.at[group], partner,
                )

    def send_rows(h):
        for i, w_ref in enumerate((q_ref, g_ref)):
            push(w_ref.at[0, :, other_columns(h)], qg.at[1, h, i], one_sem.at[QS], qr_sem.at[h], partner)

    here = set()

    def w_step(group, half, t):
        heads, plan = GROUPS[group], W_PLANS[group]
        edges = [edge for round_ in plan for edge in round_]
        way = -1 if half else 1
        whose = other if half else zl

        def block(a):
            return wraw.at[pl.ds(heads[0], len(heads)), whose, mod(y - way * a, NY)]

        def need(a):
            if (group, half, a) not in here:
                here.add((group, half, a))
                if a:
                    i = [edge[1] for edge in edges].index(a)
                    arrived(block(a), wy_recv.at[group, half, i])
                elif half:
                    arrived(block(0), wz_recv.at[group])
                else:
                    moved(block(0), wl_sem.at[group])

        if t < len(plan):
            for a, b in plan[t]:
                need(a)
                there = wy_recv.at[group, half, edges.index((a, b))]
                push(block(a), block(a), one_sem.at[WY], there, at_y(way * (b - a)))
        else:
            for _, b in edges:
                need(b)

    def to_sibling(ref):
        push(ref, ref, one_sem.at[SS], one_sem.at[SR], sibling)

    def e_first(d):
        ref = chunk(-d, 0, core)
        if d:
            arrived(ref, z_recv.at[d])
        if d == 2:
            push(ref, ref, z_send.at[4], z_recv.at[4], at_z(2))
            push(ref, ref, z_send.at[3], z_recv.at[3], at_z(1))
        if d == 6:
            push(ref, ref, z_send.at[5], z_recv.at[5], at_z(-1))
        push(ref, ref, one_sem.at[XS], xp_recv.at[d], at_x(1))
        push(ref, ref, one_sem.at[XS], xm_recv.at[d], at_x(-1))
        if d in LATE:
            push(ref, ref, one_sem.at[XS], xo_recv.at[d], at_x(2))
        to_sibling(ref)

    def e_second(d):
        ref = chunk(-d, -1, core)
        arrived(ref, xp_recv.at[d])
        if d % 2 == 0 and d not in LATE:
            push(ref, ref, one_sem.at[XS], xo_recv.at[d], at_x(1))
        to_sibling(ref)
        ref = chunk(-d, 1, core)
        arrived(ref, xm_recv.at[d])
        if d % 2 == 1 and d not in LATE:
            push(ref, ref, one_sem.at[XS], xo_recv.at[d], at_x(-1))
        to_sibling(ref)

    def e_third(d):
        ref = chunk(-d, 2, core)
        arrived(ref, xo_recv.at[d])
        to_sibling(ref)

    def each(f, *offsets):
        for d in offsets:
            f(d)

    def weights(*which):
        for group, half, t in which:
            w_step(group, half, t)

    send_weights(0)
    send_tail()
    send_chunk()
    send_weights(1)
    weights((0, 0, 0), (1, 0, 0), (2, 0, 0))
    e_first(0)
    tail_first()
    each(e_first, 1, 7)
    w_step(0, 1, 0)
    each(e_first, 2, 6)
    send_weights(2)
    w_step(0, 0, 1)
    each(e_second, 0, 1, 7)
    weights((1, 1, 0), (1, 0, 1))
    tail_second()
    send_rows(0)
    push(mult.at[0], mult.at[1], one_sem.at[MS], one_sem.at[MR], partner)
    each(e_third, 0)
    each(e_first, 3, 5, 4)
    each(e_second, 2, 6)
    weights((0, 1, 1), (2, 1, 0), (2, 0, 1))
    tail_third(1, 7)
    each(e_third, 1, 7)
    each(e_second, 3, 5)
    weights((1, 1, 1), (0, 0, 2))
    tail_third(3, 5, 4)
    for h in range(1, HEADS):
        send_rows(h)
    each(e_third, 2, 6)
    e_second(4)
    each(e_third, 3, 5, 4)
    weights((2, 1, 1), (0, 1, 2))
    arrived(ebuf.at[0], one_sem.at[SR])
    moved(qg.at[0], one_sem.at[QL])
    arrived(mult.at[1], one_sem.at[MR])

    for near in range(2):
        for c in range(BLOCKS):
            times[near, c] = jnp.broadcast_to(mult[near, pl.ds(c, 1), :], (8, TOKENS))

    for r in range(2):

        @pl.loop(0, NZH)
        def _(zz):
            part = ebuf[r, zz].reshape(NX * 2, CHUNK, ENC).astype(F32).reshape(NX * 2 * CHUNK, ENC)
            span = pl.ds(pl.multiple_of(zz * NX * 2 * CHUNK, NX * 2 * CHUNK), NX * 2 * CHUNK)
            tok[r, span, :] = part.astype(BF16)

    scale = HDIM**-0.5

    def project(h):
        @pl.loop(0, 2)
        def _(r):
            kv = jnp.dot(tok[r], wraw[h].reshape(2 * NY * WROWS, 2 * HDIM), preferred_element_type=F32).astype(BF16)
            keys[r] = kv[:, :HDIM]
            values[r] = kv[:, HDIM:]

    def nt(a, b):
        return lax.dot_general(a, b, (((1,), (1,)), ((), ())), preferred_element_type=F32)

    def tn(a, b):
        return lax.dot_general(a, b, (((0,), (0,)), ((), ())), preferred_element_type=F32)

    def attend_one(h, near):
        r = zl if near == 0 else other
        k, v = keys[r], values[r]
        q, g = qg[near, h, 0], qg[near, h, 1]
        shape = (BLOCKS, BLOCK // 8, 8, TOKENS)
        m = times[near].reshape(BLOCKS, 1, 8, TOKENS)
        scores = nt(q, k).reshape(shape) + jnp.where(m > 0.0, 0.0, -1e30)
        top = jnp.max(scores, axis=3, keepdims=True)
        weights = jnp.exp2((scores - top) * (scale * LOG2E)) * m
        probs = weights * (1.0 / jnp.sum(weights, axis=3, keepdims=True))
        dprob = nt(g, v).reshape(shape)
        delta = jnp.sum(probs * dprob, axis=3, keepdims=True)
        s = (probs * ((dprob - delta) * scale)).reshape(ROWS, TOKENS).astype(BF16)
        p = probs.reshape(ROWS, TOKENS).astype(BF16)
        stage[near, h, 0] = jnp.dot(p, v, preferred_element_type=F32).astype(BF16)
        stage[near, h, 1] = jnp.dot(s, k, preferred_element_type=F32).astype(BF16)
        slots_t[near, pl.ds(0, HDIM), :] = tn(q, s).astype(BF16)
        slots_t[near, pl.ds(HDIM, HDIM), :] = tn(g, p).astype(BF16)

    def attend(h):
        arrived(qg.at[1, h], qr_sem.at[h])
        attend_one(h, 1)
        attend_one(h, 0)
        for i, out in enumerate((ctx_out, gq_out)):
            there = out.at[0, :, own_columns(h)]
            push(stage.at[1, h, i], there, one_sem.at[OS], one_sem.at[OR], partner)
            pltpu.make_async_copy(stage.at[0, h, i], there, one_sem.at[OL]).start()

    def term(h):
        both = jnp.dot(slots_t[0], tok[zl], preferred_element_type=F32)
        both += jnp.dot(slots_t[1], tok[other], preferred_element_type=F32)
        terms[h] = both.T.reshape(2, NY, WROWS, 2 * HDIM).astype(BF16)

    def reduce(h, stage_no):
        plan = PLANS[h]
        edges = [edge for round_ in plan for edge in round_]
        for half in range(2):
            way = -1 if half else 1
            whose = other if half else zl

            def gather(whole, b, h=h, half=half, edges=edges):
                for i, edge in enumerate(edges):
                    if edge[1] == b:
                        arrived(landed.at[h, half, i], rs_recv.at[h, half, i])
                        whole += landed[h, half, i].astype(F32)
                return whole

            if stage_no < len(plan):
                for a, b in plan[stage_no]:
                    i = edges.index((a, b))
                    there = mod(y + way * a, NY)
                    if any(edge[1] == a for edge in edges):
                        terms[h, whose, there] = gather(terms[h, whose, there].astype(F32), a).astype(BF16)
                    device = across(way * a) if half and b == 0 else at_y(way * (a - b))
                    push(terms.at[h, whose, there], landed.at[h, half, i], rs_send.at[half], rs_recv.at[h, half, i], device)
                if half and stage_no == 0:
                    push(terms.at[h, other, y], landed.at[h, 1, 7], rs_send.at[1], rs_recv.at[h, 1, 7], partner)
            else:
                if half:
                    arrived(landed.at[h, 1, 7], rs_recv.at[h, 1, 7])
                    whole = landed[h, 1, 7].astype(F32)
                else:
                    whole = terms[h, zl, y].astype(F32)
                total[h, half] = gather(whole, 0)
                columns = other_columns(h) if half else own_columns(h)
                for i, out in enumerate((kg_out, vg_out)):
                    part = total.at[h, half, :, pl.ds(i * HDIM, HDIM)]
                    pltpu.make_async_copy(part, out.at[0, :, columns], one_sem.at[FL]).start()

    def sums(*which):
        for h, stage_no in which:
            reduce(h, stage_no)

    project(0)
    w_step(2, 0, 2)
    attend(0)
    w_step(2, 1, 2)
    term(0)
    reduce(0, 0)
    weights((1, 0, 2), (1, 1, 2))
    project(1)
    attend(1)
    reduce(0, 1)
    term(1)
    reduce(1, 0)
    weights((2, 0, 3), (2, 1, 3))
    project(2)
    reduce(0, 2)
    attend(2)
    reduce(1, 1)
    term(2)
    reduce(2, 0)
    reduce(0, 3)
    project(3)
    reduce(1, 2)
    attend(3)
    term(3)
    sums((3, 0), (2, 1), (1, 3), (0, 4), (3, 1), (2, 2), (1, 4), (3, 2))

    arrived(stage.at[1], one_sem.at[OR])
    moved(stage.at[0], one_sem.at[OL])
    moved(total, one_sem.at[FL])
    left(stage.at[1], one_sem.at[OS])
    left(mult.at[0], one_sem.at[MS])
    left(qg.at[1], one_sem.at[QS])
    left(wraw.at[:, 0, 0], one_sem.at[WZ])
    left(wraw.at[:, :, pl.ds(0, 7)], one_sem.at[WY])
    left(ebuf.at[0], one_sem.at[SS])
    left(ebuf.at[0, pl.ds(0, 3), :, :, :, pl.ds(0, FIRST)], one_sem.at[XS])
    left(ebuf.at[0, 0, pl.ds(0, 3), 0, :, rest], one_sem.at[BX])
    left(ebuf.at[0, :, :, 0, :, rest], one_sem.at[BZ])
    left(ebuf.at[0, pl.ds(0, 3), :, 0, :, rest], one_sem.at[BF])
    left(landed.at[:, 0, pl.ds(0, 7)], rs_send.at[0])
    left(landed.at[:, 1], rs_send.at[1])
    for d in range(1, NZ):
        left(chunk(0, 0, core), z_send.at[d])


def settle(*refs):
    ins, outs, bufs, sems = refs[:4], refs[4:8], refs[8:12], refs[12]
    inward = [pltpu.make_async_copy(a, b, sems.at[0, i]) for i, (a, b) in enumerate(zip(ins, bufs, strict=True))]
    outward = [pltpu.make_async_copy(a, b, sems.at[1, i]) for i, (a, b) in enumerate(zip(bufs, outs, strict=True))]
    for copy in inward:
        copy.start()
    for copy, later in zip(inward, outward, strict=True):
        copy.wait()
        later.start()
    for copy in outward:
        copy.wait()


def body(queries, grad_context, encodings, table, counts, key_weight, value_weight):
    any_ref = pl.BlockSpec(memory_space=pl.ANY)
    vmem = pl.BlockSpec(memory_space=pltpu.VMEM)
    smem = pl.BlockSpec(memory_space=pltpu.SMEM)
    dma = pltpu.SemaphoreType.DMA
    eight = dma((NZ,))
    local = key_weight.shape[2]
    scratch = [
        pltpu.VMEM((2, NZH, NX, 2, CHUNK, ENC), BF16),
        pltpu.VMEM((2, TOKENS, ENC), BF16),
        pltpu.VMEM((HEADS, 2, NY, WROWS, 2 * HDIM), BF16),
        pltpu.VMEM((2, HEADS, 2, ROWS, HDIM), BF16),
        pltpu.VMEM((2, 8, TOKENS), F32),
        pltpu.VMEM((2, BLOCKS, 8, TOKENS), F32),
        pltpu.VMEM((2, TOKENS, HDIM), BF16),
        pltpu.VMEM((2, TOKENS, HDIM), BF16),
        pltpu.VMEM((2, 2 * HDIM, TOKENS), BF16),
        pltpu.VMEM((HEADS, 2, NY, WROWS, 2 * HDIM), BF16),
        pltpu.VMEM((HEADS, 2, 8, WROWS, 2 * HDIM), BF16),
        pltpu.VMEM((2, HEADS, 2, ROWS, HDIM), BF16),
        pltpu.VMEM((HEADS, 2, WROWS, 2 * HDIM), F32),
        dma((16,)), eight, eight, eight, eight, eight, dma((NX,)), eight, dma((HEADS,)), dma((3,)), dma((3,)), dma((3, 2, 7)), dma((2,)),
        dma((HEADS, 2, 8)),
    ]
    outs = pl.pallas_call(
        kernel,
        out_shape=(
            jax.ShapeDtypeStruct((1, ROWS, local), BF16),
            jax.ShapeDtypeStruct((1, ROWS, local), BF16),
            jax.ShapeDtypeStruct((1, WROWS, local), F32),
            jax.ShapeDtypeStruct((1, WROWS, local), F32),
        ),
        in_specs=[vmem, smem, any_ref, any_ref, vmem, any_ref, any_ref],
        out_specs=(any_ref,) * 4,
        scratch_shapes=scratch,
        compiler_params=pltpu.CompilerParams(
            collective_id=0, has_side_effects=True, vmem_limit_bytes=56 * 1024 * 1024
        ),
    )(table.T, counts, queries, grad_context, encodings, key_weight, value_weight)
    return pl.pallas_call(
        settle,
        out_shape=tuple(jax.ShapeDtypeStruct(o.shape, o.dtype) for o in outs),
        in_specs=[any_ref] * 4,
        out_specs=(any_ref,) * 4,
        scratch_shapes=[*(pltpu.VMEM(o.shape, o.dtype) for o in outs), dma((2, 4))],
        compiler_params=pltpu.CompilerParams(vmem_limit_bytes=60 * 1024 * 1024),
    )(*outs)


def solution(mesh):
    in_specs = (
        P("section", "dp", "mp"),
        P("section", "dp", "mp"),
        P("dp", ("section", "mp"), None),
        P("dp", None),
        P("dp"),
        P("section", "dp", "mp"),
        P("section", "dp", "mp"),
    )
    out_specs = (
        P("section", "dp", "mp"),
        P("section", "dp", "mp"),
        P("section", "dp", "mp"),
        P("section", "dp", "mp"),
    )
    return jax.shard_map(body, mesh=mesh, in_specs=in_specs, out_specs=out_specs, check_vma=False)
```

```python
import functools

import jax
import jax.numpy as jnp
from jax import lax
from jax.experimental import pallas as pl
from jax.experimental.pallas import tpu as pltpu
from jax.sharding import PartitionSpec as P

MESH = pl.DeviceIdType.MESH
F32, BF16 = jnp.float32, jnp.bfloat16
HDIM = 128
LOG2E = 1.4426950408889634
NY, NX, NZH, NZ = 8, 4, 4, 8
HEADS = 4
SLOTS, PIECE, ENC = 6, 4, 896
CHUNK = SLOTS * PIECE
TOKENS = 768
ROWS, BLOCK, BLOCKS = 192, 64, 3
WROWS = 56
GROUPS = ((0,), (1,), (2, 3))
GROUP_OF = (0, 1, 2, 2)
W_TWO = (((0, 2), (0, -2), (0, 1), (0, -1)), ((2, 4), (2, 3), (-2, -3)))
W_THREE = (((0, 1), (0, -1)), ((1, 3), (1, 2), (-1, -2)), ((3, 4), (-2, -3)))
W_PLANS = (W_TWO, W_TWO, W_THREE)
RING = (((4, 3), (-3, -2)), ((3, 2), (-2, -1)), ((2, 1), (-1, 0)), ((1, 0),))
TWO = (((4, 2), (3, 2), (-3, -2), (1, 0), (-1, 0)), ((2, 0), (-2, 0)))
PLANS = (RING, RING, TWO, TWO)
QL, QS, MS, MR, WZ, WY, SS, SR, XS, OL, OS, OR, FL, BX, BZ, BF = range(16)
FIRST = 640
LATE = (3, 4, 5)


def mod(value, n):
    return lax.rem(value + n, n)


def kernel(
    table_ref, counts_ref, q_ref, g_ref, enc_ref, wk_ref, wv_ref,
    ctx_out, gq_out, kg_out, vg_out,
    ebuf, tok, wraw, qg, mult, times, keys, values, slots_t, terms, landed, stage, total,
    one_sem, z_send, z_recv, xp_recv, xm_recv, xo_recv, bx_recv, bz_recv, qr_sem, wl_sem, wz_recv, wy_recv, rs_send, rs_recv,
):
    dp, section, zh = lax.axis_index("dp"), lax.axis_index("section"), lax.axis_index("mp")
    zl, y = dp // NY, lax.rem(dp, NY)
    x, core = section // 2, lax.rem(section, 2)
    z = zh * 2 + zl
    other = 1 - zl

    partner = {"dp": other * NY + y}
    sibling = {"section": x * 2 + 1 - core}

    def at_y(step):
        return {"dp": zl * NY + mod(y + step, NY)}

    def across(step):
        return {"dp": other * NY + mod(y + step, NY)}

    def at_x(step):
        return {"section": mod(x + step, NX) * 2 + core}

    def at_z(step):
        there = mod(z + step, NZ)
        return {"dp": lax.rem(there, 2) * NY + y, "mp": there // 2}

    def remote(src, dst, send, recv, device):
        return pltpu.make_async_remote_copy(
            src_ref=src, dst_ref=dst, send_sem=send, recv_sem=recv, device_id=device, device_id_type=MESH
        )

    def push(src, dst, send, recv, device):
        remote(src, dst, send, recv, device).start()

    def arrived(ref, recv):
        remote(ref, ref, recv, recv, sibling).wait_recv()

    def left(ref, send):
        remote(ref, ref, send, send, sibling).wait_send()

    def moved(ref, sem):
        pltpu.make_async_copy(ref, ref, sem).wait()

    barrier = pltpu.get_barrier_semaphore()
    friends = [at_z(d) for d in (1, -1, 2, -2)] + [at_x(d) for d in (1, -1, 2)] + [sibling]
    friends += [at_y(d) for d in (1, -1, 2, -2)] + [across(d) for d in (1, -1, 2, -2)]
    for friend in friends:
        pl.semaphore_signal(barrier, inc=1, device_id=friend, device_id_type=MESH)

    def own_columns(h):
        return pl.ds(pl.multiple_of(zl * HEADS * HDIM + h * HDIM, HDIM), HDIM)

    def other_columns(h):
        return pl.ds(pl.multiple_of(other * HEADS * HDIM + h * HDIM, HDIM), HDIM)

    for h in range(HEADS):
        for i, w_ref in enumerate((wk_ref, wv_ref)):
            there = wraw.at[h, zl, y, :, pl.ds(i * HDIM, HDIM)]
            pltpu.make_async_copy(w_ref.at[0, :, own_columns(h)], there, wl_sem.at[GROUP_OF[h]]).start()
    for h in range(HEADS):
        for i, w_ref in enumerate((q_ref, g_ref)):
            pltpu.make_async_copy(w_ref.at[0, :, own_columns(h)], qg.at[0, h, i], one_sem.at[QL]).start()
    pieces = [enc_ref[s].astype(F32) for s in range(SLOTS)]
    ebuf[zl, zh, x, core] = jnp.concatenate(pieces, axis=0).astype(BF16)
    token = lax.broadcasted_iota(jnp.int32, (8, TOKENS), 1)
    slot_of = (token - CHUNK * ((token * 2731) >> 16)) >> 2
    row = lax.broadcasted_iota(jnp.int32, (8, TOKENS), 0)
    compact = jnp.zeros((8, TOKENS), F32)
    for c in range(BLOCKS):
        first = jnp.where(slot_of == table_ref[pl.ds(0, 1), pl.ds(c, 1)], 1.0, 0.0)
        second = jnp.where(slot_of == table_ref[pl.ds(1, 1), pl.ds(c, 1)], 1.0, 0.0)
        both = first + second * jnp.where(counts_ref[c] > 1, 1.0, 0.0)
        compact = jnp.where(row == c, both, compact)
    mult[0] = compact

    pl.semaphore_wait(barrier, len(friends))

    def chunk(dz, dx, core_of):
        zz = mod(z + dz, NZ)
        return ebuf.at[lax.rem(zz, 2), zz // 2, mod(x + dx, NX), core_of, :, pl.ds(0, FIRST)]

    rest = pl.ds(FIRST, ENC - FIRST)

    def tail_of(dx):
        return ebuf.at[zl, zh, mod(x + dx, NX), core, :, rest]

    def tails(dz):
        zz = mod(z + dz, NZ)
        return ebuf.at[lax.rem(zz, 2), zz // 2, :, core, :, rest]

    mine = chunk(0, 0, core)

    def send_chunk():
        for d in (1, 7, 2, 6):
            push(mine, mine, z_send.at[d], z_recv.at[d], at_z(d if d < 4 else d - NZ))

    def send_tail():
        for dx in (1, -1, 2):
            push(tail_of(0), tail_of(0), one_sem.at[BX], bx_recv.at[dx % NX], at_x(dx))

    def tail_first():
        for dx in (1, 2, 3):
            arrived(tail_of(-dx), bx_recv.at[dx])
        for d in (2, 6, 1, 7):
            push(tails(0), tails(0), one_sem.at[BZ], bz_recv.at[d], at_z(d if d < 4 else d - NZ))
        to_sibling(tails(0))

    def tail_second():
        arrived(tails(-2), bz_recv.at[2])
        push(tails(-2), tails(-2), one_sem.at[BF], bz_recv.at[4], at_z(2))
        push(tails(-2), tails(-2), one_sem.at[BF], bz_recv.at[3], at_z(1))
        arrived(tails(2), bz_recv.at[6])
        push(tails(2), tails(2), one_sem.at[BF], bz_recv.at[5], at_z(-1))
        for d in (2, 6):
            to_sibling(tails(-d))

    def tail_third(*which):
        for d in which:
            arrived(tails(-d), bz_recv.at[d])
            to_sibling(tails(-d))

    def send_weights(group):
        for h in GROUPS[group]:
            for i, w_ref in enumerate((wk_ref, wv_ref)):
                push(
                    w_ref.at[0, :, other_columns(h)], wraw.at[h, zl, y, :, pl.ds(i * HDIM, HDIM)],
                    one_sem.at[WZ], wz_recv.at[group], partner,
                )

    def send_rows(h):
        for i, w_ref in enumerate((q_ref, g_ref)):
            push(w_ref.at[0, :, other_columns(h)], qg.at[1, h, i], one_sem.at[QS], qr_sem.at[h], partner)

    here = set()

    def w_step(group, half, t):
        heads, plan = GROUPS[group], W_PLANS[group]
        edges = [edge for round_ in plan for edge in round_]
        way = -1 if half else 1
        whose = other if half else zl

        def block(a):
            return wraw.at[pl.ds(heads[0], len(heads)), whose, mod(y - way * a, NY)]

        def need(a):
            if (group, half, a) not in here:
                here.add((group, half, a))
                if a:
                    i = [edge[1] for edge in edges].index(a)
                    arrived(block(a), wy_recv.at[group, half, i])
                elif half:
                    arrived(block(0), wz_recv.at[group])
                else:
                    moved(block(0), wl_sem.at[group])

        if t < len(plan):
            for a, b in plan[t]:
                need(a)
                there = wy_recv.at[group, half, edges.index((a, b))]
                push(block(a), block(a), one_sem.at[WY], there, at_y(way * (b - a)))
        else:
            for _, b in edges:
                need(b)

    def to_sibling(ref):
        push(ref, ref, one_sem.at[SS], one_sem.at[SR], sibling)

    def e_first(d):
        ref = chunk(-d, 0, core)
        if d:
            arrived(ref, z_recv.at[d])
        if d == 2:
            push(ref, ref, z_send.at[4], z_recv.at[4], at_z(2))
            push(ref, ref, z_send.at[3], z_recv.at[3], at_z(1))
        if d == 6:
            push(ref, ref, z_send.at[5], z_recv.at[5], at_z(-1))
        push(ref, ref, one_sem.at[XS], xp_recv.at[d], at_x(1))
        push(ref, ref, one_sem.at[XS], xm_recv.at[d], at_x(-1))
        if d in LATE:
            push(ref, ref, one_sem.at[XS], xo_recv.at[d], at_x(2))
        to_sibling(ref)

    def e_second(d):
        ref = chunk(-d, -1, core)
        arrived(ref, xp_recv.at[d])
        if d % 2 == 0 and d not in LATE:
            push(ref, ref, one_sem.at[XS], xo_recv.at[d], at_x(1))
        to_sibling(ref)
        ref = chunk(-d, 1, core)
        arrived(ref, xm_recv.at[d])
        if d % 2 == 1 and d not in LATE:
            push(ref, ref, one_sem.at[XS], xo_recv.at[d], at_x(-1))
        to_sibling(ref)

    def e_third(d):
        ref = chunk(-d, 2, core)
        arrived(ref, xo_recv.at[d])
        to_sibling(ref)

    def each(f, *offsets):
        for d in offsets:
            f(d)

    def weights(*which):
        for group, half, t in which:
            w_step(group, half, t)

    send_weights(0)
    send_tail()
    send_chunk()
    send_weights(1)
    weights((0, 0, 0), (1, 0, 0), (2, 0, 0))
    e_first(0)
    tail_first()
    each(e_first, 1, 7)
    w_step(0, 1, 0)
    each(e_first, 2, 6)
    send_weights(2)
    w_step(0, 0, 1)
    each(e_second, 0, 1, 7)
    weights((1, 1, 0), (1, 0, 1))
    tail_second()
    send_rows(0)
    push(mult.at[0], mult.at[1], one_sem.at[MS], one_sem.at[MR], partner)
    each(e_third, 0)
    each(e_first, 3, 5, 4)
    each(e_second, 2, 6)
    weights((0, 1, 1), (2, 1, 0), (2, 0, 1))
    tail_third(1, 7)
    each(e_third, 1, 7)
    w_step(1, 1, 1)
    each(e_second, 3, 5)
    w_step(0, 0, 2)
    tail_third(3, 5, 4)
    for h in range(1, HEADS):
        send_rows(h)
    each(e_third, 2, 6)
    e_second(4)
    each(e_third, 3, 5, 4)
    weights((2, 1, 1), (0, 1, 2))
    arrived(ebuf.at[0], one_sem.at[SR])
    moved(qg.at[0], one_sem.at[QL])
    arrived(mult.at[1], one_sem.at[MR])

    for near in range(2):
        for c in range(BLOCKS):
            times[near, c] = jnp.broadcast_to(mult[near, pl.ds(c, 1), :], (8, TOKENS))

    for r in range(2):

        @pl.loop(0, NZH)
        def _(zz):
            part = ebuf[r, zz].reshape(NX * 2, CHUNK, ENC).astype(F32).reshape(NX * 2 * CHUNK, ENC)
            span = pl.ds(pl.multiple_of(zz * NX * 2 * CHUNK, NX * 2 * CHUNK), NX * 2 * CHUNK)
            tok[r, span, :] = part.astype(BF16)

    scale = HDIM**-0.5

    def project(h):
        @pl.loop(0, 2)
        def _(r):
            kv = jnp.dot(tok[r], wraw[h].reshape(2 * NY * WROWS, 2 * HDIM), preferred_element_type=F32).astype(BF16)
            keys[r] = kv[:, :HDIM]
            values[r] = kv[:, HDIM:]

    def nt(a, b):
        return lax.dot_general(a, b, (((1,), (1,)), ((), ())), preferred_element_type=F32)

    def tn(a, b):
        return lax.dot_general(a, b, (((0,), (0,)), ((), ())), preferred_element_type=F32)

    def attend_one(h, near):
        r = zl if near == 0 else other
        k, v = keys[r], values[r]
        q, g = qg[near, h, 0], qg[near, h, 1]
        shape = (BLOCKS, BLOCK // 8, 8, TOKENS)
        m = times[near].reshape(BLOCKS, 1, 8, TOKENS)
        scores = nt(q, k).reshape(shape) + jnp.where(m > 0.0, 0.0, -1e30)
        top = jnp.max(scores, axis=3, keepdims=True)
        weights = jnp.exp2((scores - top) * (scale * LOG2E)) * m
        probs = weights * (1.0 / jnp.sum(weights, axis=3, keepdims=True))
        dprob = nt(g, v).reshape(shape)
        delta = jnp.sum(probs * dprob, axis=3, keepdims=True)
        s = (probs * ((dprob - delta) * scale)).reshape(ROWS, TOKENS).astype(BF16)
        p = probs.reshape(ROWS, TOKENS).astype(BF16)
        stage[near, h, 0] = jnp.dot(p, v, preferred_element_type=F32).astype(BF16)
        stage[near, h, 1] = jnp.dot(s, k, preferred_element_type=F32).astype(BF16)
        slots_t[near, pl.ds(0, HDIM), :] = tn(q, s).astype(BF16)
        slots_t[near, pl.ds(HDIM, HDIM), :] = tn(g, p).astype(BF16)

    def attend(h):
        arrived(qg.at[1, h], qr_sem.at[h])
        attend_one(h, 1)
        attend_one(h, 0)
        for i, out in enumerate((ctx_out, gq_out)):
            there = out.at[0, :, own_columns(h)]
            push(stage.at[1, h, i], there, one_sem.at[OS], one_sem.at[OR], partner)
            pltpu.make_async_copy(stage.at[0, h, i], there, one_sem.at[OL]).start()

    def term(h):
        both = jnp.dot(slots_t[0], tok[zl], preferred_element_type=F32)
        both += jnp.dot(slots_t[1], tok[other], preferred_element_type=F32)
        terms[h] = both.T.reshape(2, NY, WROWS, 2 * HDIM).astype(BF16)

    def reduce(h, stage_no):
        plan = PLANS[h]
        edges = [edge for round_ in plan for edge in round_]
        for half in range(2):
            way = -1 if half else 1
            whose = other if half else zl

            def gather(whole, b, h=h, half=half, edges=edges):
                for i, edge in enumerate(edges):
                    if edge[1] == b:
                        arrived(landed.at[h, half, i], rs_recv.at[h, half, i])
                        whole += landed[h, half, i].astype(F32)
                return whole

            if stage_no < len(plan):
                for a, b in plan[stage_no]:
                    i = edges.index((a, b))
                    there = mod(y + way * a, NY)
                    if any(edge[1] == a for edge in edges):
                        terms[h, whose, there] = gather(terms[h, whose, there].astype(F32), a).astype(BF16)
                    device = across(way * a) if half and b == 0 else at_y(way * (a - b))
                    push(terms.at[h, whose, there], landed.at[h, half, i], rs_send.at[half], rs_recv.at[h, half, i], device)
                if half and stage_no == 0:
                    push(terms.at[h, other, y], landed.at[h, 1, 7], rs_send.at[1], rs_recv.at[h, 1, 7], partner)
            else:
                if half:
                    arrived(landed.at[h, 1, 7], rs_recv.at[h, 1, 7])
                    whole = landed[h, 1, 7].astype(F32)
                else:
                    whole = terms[h, zl, y].astype(F32)
                total[h, half] = gather(whole, 0)
                columns = other_columns(h) if half else own_columns(h)
                for i, out in enumerate((kg_out, vg_out)):
                    part = total.at[h, half, :, pl.ds(i * HDIM, HDIM)]
                    pltpu.make_async_copy(part, out.at[0, :, columns], one_sem.at[FL]).start()

    def sums(*which):
        for h, stage_no in which:
            reduce(h, stage_no)

    project(0)
    w_step(2, 0, 2)
    attend(0)
    w_step(2, 1, 2)
    term(0)
    reduce(0, 0)
    weights((1, 0, 2), (1, 1, 2))
    project(1)
    attend(1)
    reduce(0, 1)
    term(1)
    reduce(1, 0)
    weights((2, 0, 3), (2, 1, 3))
    project(2)
    reduce(0, 2)
    attend(2)
    reduce(1, 1)
    term(2)
    reduce(2, 0)
    reduce(0, 3)
    project(3)
    reduce(1, 2)
    attend(3)
    term(3)
    sums((3, 0), (2, 1), (1, 3), (0, 4), (3, 1), (2, 2), (1, 4), (3, 2))

    arrived(stage.at[1], one_sem.at[OR])
    moved(stage.at[0], one_sem.at[OL])
    moved(total, one_sem.at[FL])
    left(stage.at[1], one_sem.at[OS])
    left(mult.at[0], one_sem.at[MS])
    left(qg.at[1], one_sem.at[QS])
    left(wraw.at[:, 0, 0], one_sem.at[WZ])
    left(wraw.at[:, :, pl.ds(0, 7)], one_sem.at[WY])
    left(ebuf.at[0], one_sem.at[SS])
    left(ebuf.at[0, pl.ds(0, 3), :, :, :, pl.ds(0, FIRST)], one_sem.at[XS])
    left(ebuf.at[0, 0, pl.ds(0, 3), 0, :, rest], one_sem.at[BX])
    left(ebuf.at[0, :, :, 0, :, rest], one_sem.at[BZ])
    left(ebuf.at[0, pl.ds(0, 3), :, 0, :, rest], one_sem.at[BF])
    left(landed.at[:, 0, pl.ds(0, 7)], rs_send.at[0])
    left(landed.at[:, 1], rs_send.at[1])
    for d in range(1, NZ):
        left(chunk(0, 0, core), z_send.at[d])


def settle(*refs):
    ins, outs, bufs, sems = refs[:4], refs[4:8], refs[8:12], refs[12]
    inward = [pltpu.make_async_copy(a, b, sems.at[0, i]) for i, (a, b) in enumerate(zip(ins, bufs, strict=True))]
    outward = [pltpu.make_async_copy(a, b, sems.at[1, i]) for i, (a, b) in enumerate(zip(bufs, outs, strict=True))]
    for copy in inward:
        copy.start()
    for copy, later in zip(inward, outward, strict=True):
        copy.wait()
        later.start()
    for copy in outward:
        copy.wait()


def body(queries, grad_context, encodings, table, counts, key_weight, value_weight):
    any_ref = pl.BlockSpec(memory_space=pl.ANY)
    vmem = pl.BlockSpec(memory_space=pltpu.VMEM)
    smem = pl.BlockSpec(memory_space=pltpu.SMEM)
    dma = pltpu.SemaphoreType.DMA
    eight = dma((NZ,))
    local = key_weight.shape[2]
    scratch = [
        pltpu.VMEM((2, NZH, NX, 2, CHUNK, ENC), BF16),
        pltpu.VMEM((2, TOKENS, ENC), BF16),
        pltpu.VMEM((HEADS, 2, NY, WROWS, 2 * HDIM), BF16),
        pltpu.VMEM((2, HEADS, 2, ROWS, HDIM), BF16),
        pltpu.VMEM((2, 8, TOKENS), F32),
        pltpu.VMEM((2, BLOCKS, 8, TOKENS), F32),
        pltpu.VMEM((2, TOKENS, HDIM), BF16),
        pltpu.VMEM((2, TOKENS, HDIM), BF16),
        pltpu.VMEM((2, 2 * HDIM, TOKENS), BF16),
        pltpu.VMEM((HEADS, 2, NY, WROWS, 2 * HDIM), BF16),
        pltpu.VMEM((HEADS, 2, 8, WROWS, 2 * HDIM), BF16),
        pltpu.VMEM((2, HEADS, 2, ROWS, HDIM), BF16),
        pltpu.VMEM((HEADS, 2, WROWS, 2 * HDIM), F32),
        dma((16,)), eight, eight, eight, eight, eight, dma((NX,)), eight, dma((HEADS,)), dma((3,)), dma((3,)), dma((3, 2, 7)), dma((2,)),
        dma((HEADS, 2, 8)),
    ]
    outs = pl.pallas_call(
        kernel,
        out_shape=(
            jax.ShapeDtypeStruct((1, ROWS, local), BF16),
            jax.ShapeDtypeStruct((1, ROWS, local), BF16),
            jax.ShapeDtypeStruct((1, WROWS, local), F32),
            jax.ShapeDtypeStruct((1, WROWS, local), F32),
        ),
        in_specs=[vmem, smem, any_ref, any_ref, vmem, any_ref, any_ref],
        out_specs=(any_ref,) * 4,
        scratch_shapes=scratch,
        compiler_params=pltpu.CompilerParams(
            collective_id=0, has_side_effects=True, vmem_limit_bytes=56 * 1024 * 1024
        ),
    )(table.T, counts, queries, grad_context, encodings, key_weight, value_weight)
    return pl.pallas_call(
        settle,
        out_shape=tuple(jax.ShapeDtypeStruct(o.shape, o.dtype) for o in outs),
        in_specs=[any_ref] * 4,
        out_specs=(any_ref,) * 4,
        scratch_shapes=[*(pltpu.VMEM(o.shape, o.dtype) for o in outs), dma((2, 4))],
        compiler_params=pltpu.CompilerParams(vmem_limit_bytes=60 * 1024 * 1024),
    )(*outs)


def solution(mesh):
    in_specs = (
        P("section", "dp", "mp"),
        P("section", "dp", "mp"),
        P("dp", ("section", "mp"), None),
        P("dp", None),
        P("dp"),
        P("section", "dp", "mp"),
        P("section", "dp", "mp"),
    )
    out_specs = (
        P("section", "dp", "mp"),
        P("section", "dp", "mp"),
        P("section", "dp", "mp"),
        P("section", "dp", "mp"),
    )
    return jax.shard_map(body, mesh=mesh, in_specs=in_specs, out_specs=out_specs, check_vma=False)
```
